32 devices in a mesh: seq: 4 (over z), batch: 4 (over y, x), mp: 2 (over core).
Axes of the slice: x: 2, y: 2, z: 4, core: 2. Of those that a mesh axis runs over, the one named last changes fastest.
Arguments:
- tokens_in: bfloat16 [8, 1024, 2048], P('batch', 'seq'), may hold values from -6 to 6
- grad_out: bfloat16 [8, 1024, 2048], P('batch', 'seq'), may hold values from -6 to 6
- w_input: bfloat16 [2048, 2048], P(('seq', 'batch'), 'mp'), may hold values from -0.125 to 0.125
- w_forget: bfloat16 [2048, 2048], P(('seq', 'batch'), 'mp'), may hold values from -0.125 to 0.125
- w_outgate: bfloat16 [2048, 2048], P(('seq', 'batch'), 'mp'), may hold values from -0.125 to 0.125
- w_out: bfloat16 [2048, 2048], P('mp', ('seq', 'batch')), may hold values from -0.25 to 0.25
- mlp_gate: bfloat16 [2048, 5632], P(('seq', 'batch'), 'mp'), may hold values from -0.125 to 0.125
- mlp_up: bfloat16 [2048, 5632], P(('seq', 'batch'), 'mp'), may hold values from -0.125 to 0.125
- mlp_down: bfloat16 [5632, 2048], P('mp', ('seq', 'batch')), may hold values from -0.15625 to 0.15625
- gain_mixer: bfloat16 [2048], replicated, may hold values from 0.25 to 1.75
- gain_mlp: bfloat16 [2048], replicated, may hold values from 0.25 to 1.75
- gain_state: bfloat16 [2048], P('mp'), may hold values from 0.25 to 1.75
- bound_param: float32 [24, 2048], P(None, 'mp'), may hold values from -12 to 2
- layer_index: int32 [1], replicated, may hold values from 18 to 23
- doc_lengths: int32 [8, 4], P('batch'), may hold values from 1 to 1024, as said below
Outputs:
- tokens_out: bfloat16 [8, 1024, 2048], P('batch', 'seq', 'mp')
- grad_in: float32 [8, 1024, 2048], P('batch', 'seq')
- grad_w_input: float32 [2048, 2048], P(('seq', 'batch'), 'mp')
- grad_w_forget: float32 [2048, 2048], P(('seq', 'batch'), 'mp')
- grad_w_outgate: float32 [2048, 2048], P(('seq', 'batch'), 'mp')
- grad_w_out: float32 [2048, 2048], P('mp', ('seq', 'batch'))
- grad_mlp_gate: float32 [2048, 5632], P(('seq', 'batch'), 'mp')
- grad_mlp_up: float32 [2048, 5632], P(('seq', 'batch'), 'mp')
- grad_mlp_down: float32 [5632, 2048], P('mp', ('seq', 'batch'))
- grad_gain_mixer: float32 [2048], P('mp')
- grad_gain_mlp: float32 [2048], P('mp')
- grad_gain_state: float32 [2048], P('mp')
- grad_bound_param: float32 [24, 2048], P(None, 'mp')
The draws below stay inside these ranges and needn't reach their ends.
Inputs may be any that keep to these rules, and one draw needn't show every extreme that they name: `doc_lengths`: each row's lengths sum to 1024; in every row one document starts within the row's first 256 tokens and ends within its last 256.
All inputs are finite; a program needn't handle non-finite values.
Results may differ from the reference program's by a relative error of at most 0.013.
Values may be sent and summed in bfloat16 or wider, within the bound.
No kernel may reach another device: no remote copies, remote signals or barrier semaphores. Data moves between devices by JAX's collectives and lax.ppermute only.
A program may use at most 256 MiB of HBM per device.

```python
import math
import jax
import jax.numpy as jnp
from jax import lax

D = 2048
FF = 5632
LAYERS = 24
TSEG = 256
DOCS = 4
ROWS = 8
SEQ_LEN = 1024


def draw_doc_lengths(key, part):
    key = jax.random.fold_in(key, 7)
    short_key, place_key = jax.random.split(key)
    shorts = jax.random.randint(short_key, (ROWS, DOCS), 1, max(2, TSEG // DOCS + 1))
    long_place = jax.random.randint(place_key, (ROWS, 1), 0, DOCS)
    is_long = jnp.arange(DOCS)[None, :] == long_place
    shorts = jnp.where(is_long, 0, shorts)
    remain = SEQ_LEN - jnp.sum(shorts, axis=1, keepdims=True)
    return jnp.where(is_long, remain, shorts).astype(jnp.int32)


def draw_bound_param(key, part):
    key = jax.random.fold_in(key, 11)
    noise_key, pick_key, slow_key, fast_key = jax.random.split(key, 4)
    layer_rows = jnp.arange(LAYERS)[:, None]
    outer_rows = jnp.logical_or(layer_rows == 0, layer_rows >= LAYERS - 6)
    noise = 0.5 * jnp.clip(jax.random.normal(noise_key, (LAYERS, D), jnp.float32), -3.0, 3.0)
    slow_share = 0.5
    slow = jax.random.bernoulli(pick_key, slow_share, (D,))
    reach = jnp.exp(jax.random.uniform(slow_key, (D,), jnp.float32, math.log(5.0), math.log(12.0)))
    slow_drop = jnp.log(jnp.float32(SEQ_LEN) / reach)
    fast_drop = jax.random.uniform(fast_key, (D,), jnp.float32, 0.0, 0.5)
    drop = jnp.where(slow, slow_drop, fast_drop)
    return jnp.where(outer_rows, noise - drop[None, :], noise).astype(jnp.float32)


def levels(own_key, dims, pieces, low, largest):
    factor_of, own = 1.0, jax.random.fold_in(own_key, 6)
    for dim, shards_of in pieces:
        draws = jnp.exp(jax.random.uniform(jax.random.fold_in(own, dim), (shards_of,), jnp.float32, low / len(pieces), largest / len(pieces)))
        factor_of = factor_of * jnp.repeat(draws, dims[dim] // shards_of).reshape([-1 if axis == dim else 1 for axis in range(len(dims))])
    return factor_of


def gaussian(key, shape, spread, most, cuts=(), kind=jnp.bfloat16):
    array = spread * jax.random.normal(key, shape, jnp.float32)
    if cuts:
        array = array * levels(key, shape, cuts, -0.22, 0.18)
    return jnp.clip(array, -most, most).astype(kind)


def setup_inputs(seed: int = 0) -> dict:
    arg_keys = jax.random.split(jax.random.key(seed), 16)
    return {
        "tokens_in": gaussian(arg_keys[0], (ROWS, SEQ_LEN, D), 1.0, 6.0, ((0, 4), (1, 4))),
        "grad_out": gaussian(arg_keys[1], (ROWS, SEQ_LEN, D), 1.0, 6.0, ((0, 4), (1, 4))),
        "w_input": gaussian(arg_keys[2], (D, D), D ** -0.5, 0.125, ((0, 16), (1, 2))),
        "w_forget": gaussian(arg_keys[3], (D, D), D ** -0.5, 0.125, ((0, 16), (1, 2))),
        "w_outgate": gaussian(arg_keys[4], (D, D), D ** -0.5, 0.125, ((0, 16), (1, 2))),
        "w_out": gaussian(arg_keys[5], (D, D), (D // 4) ** -0.5, 0.25, ((0, 2), (1, 16))),
        "mlp_gate": gaussian(arg_keys[6], (D, FF), D ** -0.5, 0.125, ((0, 16), (1, 2))),
        "mlp_up": gaussian(arg_keys[7], (D, FF), D ** -0.5, 0.125, ((0, 16), (1, 2))),
        "mlp_down": gaussian(arg_keys[8], (FF, D), (FF // 4) ** -0.5, 0.15625, ((0, 2), (1, 16))),
        "gain_mixer": jnp.clip(1.0 + 0.15 * jax.random.normal(arg_keys[9], (D,), jnp.float32), 0.25, 1.75).astype(jnp.bfloat16),
        "gain_mlp": jnp.clip(1.0 + 0.15 * jax.random.normal(arg_keys[10], (D,), jnp.float32), 0.25, 1.75).astype(jnp.bfloat16),
        "gain_state": jnp.clip(1.0 + 0.15 * jax.random.normal(arg_keys[11], (D,), jnp.float32), 0.25, 1.75).astype(jnp.bfloat16),
        "bound_param": draw_bound_param(jax.random.fold_in(arg_keys[15], 71), 0),
        "layer_index": jax.random.randint(arg_keys[13], (1,), LAYERS - 6, LAYERS).astype(jnp.int32),
        "doc_lengths": draw_doc_lengths(jax.random.fold_in(arg_keys[15], 71), 0),
    }


EPSILON = 1e-06

@jax.custom_vjp
def low(v):
    return lax.optimization_barrier(v.astype(jnp.bfloat16)).astype(jnp.float32)

@jax.custom_vjp
def low_back(v):
    return v

def low_keep(v):
    return (low(v), None)

def low_pass(kept, grad):
    return (grad,)

def back_keep(v):
    return (v, None)

def back_low(kept, grad):
    return (low(grad),)
low.defvjp(low_keep, low_pass)
low_back.defvjp(back_keep, back_low)

def matmul(left, right):
    return jnp.dot(left, right, precision=lax.Precision.HIGHEST, preferred_element_type=jnp.float32)

def rms_scale(values, scale):
    return values * lax.rsqrt(lax.optimization_barrier(jnp.mean(values * values, axis=-1, keepdims=True)) + EPSILON) * scale

def lower_bound(bound_param, layer_index):
    weights = jax.nn.softmax(bound_param, axis=0)
    running = jnp.cumsum(weights, axis=0)
    return lax.dynamic_index_in_dim(running, layer_index[0], 0, keepdims=False) - weights[0]

def recurrence(decay, inputs):
    blocks = decay.shape[0] // TSEG
    width = decay.shape[1]

    def block_run(state, pair):

        def advance(inner, terms):
            inner = terms[0] * inner + terms[1]
            return (inner, inner)
        return lax.scan(advance, state, pair)
    final, states = lax.scan(jax.checkpoint(block_run), jnp.zeros((width,), jnp.float32), (decay.reshape(blocks, TSEG, width), inputs.reshape(blocks, TSEG, width)))
    return states.reshape(decay.shape)

def layer_row(tok_row, reset_row, layer_index, w_input, w_forget, w_outgate, w_out, mlp_gate, mlp_up, mlp_down, gain_mixer, gain_mlp, gain_state, bound_param):
    bound = lower_bound(bound_param, layer_index)
    normed_in = low(rms_scale(tok_row, gain_mixer))
    proj_in = low_back(matmul(normed_in, w_input))
    proj_forget = low_back(matmul(normed_in, w_forget))
    proj_gate = low_back(matmul(normed_in, w_outgate))
    forget = bound + (1.0 - bound) * jax.nn.sigmoid(proj_forget)
    inputs = jax.nn.silu(proj_in) * (1.0 - forget)
    decay = forget * (1.0 - reset_row[:, None])
    states = recurrence(decay, inputs)
    gated = low(rms_scale(states, gain_state) * jax.nn.silu(proj_gate))
    mixed = low_back(matmul(gated, w_out))
    resid = tok_row + mixed
    normed_mlp = low(rms_scale(resid, gain_mlp))
    gate_act = low_back(matmul(normed_mlp, mlp_gate))
    up_act = low_back(matmul(normed_mlp, mlp_up))
    hidden = low(jax.nn.silu(gate_act) * up_act)
    return resid + low_back(matmul(hidden, mlp_down))

def reference(tokens_in, grad_out, w_input, w_forget, w_outgate, w_out, mlp_gate, mlp_up, mlp_down, gain_mixer, gain_mlp, gain_state, bound_param, layer_index, doc_lengths):
    params = tuple((p.astype(jnp.float32) for p in (w_input, w_forget, w_outgate, w_out, mlp_gate, mlp_up, mlp_down, gain_mixer, gain_mlp, gain_state))) + (bound_param,)
    starts = jnp.cumsum(doc_lengths, axis=1) - doc_lengths
    places = jnp.arange(SEQ_LEN, dtype=jnp.int32)
    resets = jnp.any(places[None, :, None] == starts[:, None, :], axis=2).astype(jnp.float32)

    def one_row(totals, item):
        tok_row, cot_row, reset_row = item

        def forward(tok_value, *weights):
            return layer_row(tok_value, reset_row, layer_index, *weights)
        result, pull = jax.vjp(forward, tok_row, *params)
        grads = pull(cot_row)
        totals = tuple((total + grad for total, grad in zip(totals, grads[1:])))
        return (totals, (result.astype(jnp.bfloat16), grads[0]))
    start_totals = tuple((jnp.zeros(p.shape, jnp.float32) for p in params))
    totals, outputs = lax.scan(one_row, start_totals, (tokens_in.astype(jnp.float32), grad_out.astype(jnp.float32), resets))
    return (outputs[0], outputs[1], totals[0], totals[1], totals[2], totals[3], totals[4], totals[5], totals[6], totals[7], totals[8], totals[9], totals[10])
```

```python
import functools

import jax
import jax.numpy as jnp
from jax import lax
from jax.experimental import pallas as pl
from jax.experimental.pallas import tpu as pltpu
from jax.sharding import PartitionSpec as P

EPSILON = 1e-06
LOW = jnp.bfloat16


def swap_x(v):
    return lax.ppermute(v, "batch", [(i, i ^ 1) for i in range(4)])


def swap_y(v):
    return lax.ppermute(v, "batch", [(i, i ^ 2) for i in range(4)])


def swap_xy(v):
    return lax.ppermute(v, "batch", [(i, i ^ 3) for i in range(4)])


def swap_core(v):
    return lax.ppermute(v, "mp", [(0, 1), (1, 0)])


def plain_dot(left, right):
    return jnp.dot(left, right, preferred_element_type=jnp.float32)


def left_dot(left, right):
    return lax.dot_general(
        left, right, (((0,), (0,)), ((), ())), preferred_element_type=jnp.float32
    )


def right_dot(left, right):
    return lax.dot_general(
        left, right, (((1,), (1,)), ((), ())), preferred_element_type=jnp.float32
    )


def norm_back(upstream, values, scale, inverse):
    weighted = upstream * scale
    return inverse * weighted - values * inverse**3 * jnp.mean(
        weighted * values, axis=-1, keepdims=True
    )


def by_place(blocks, batch):
    stacked = jnp.stack(blocks)
    return [
        lax.dynamic_index_in_dim(stacked, jnp.bitwise_xor(batch, a), 0, keepdims=False)
        for a in range(4)
    ]


def exchange(blocks):
    return [blocks[0], swap_x(blocks[1]), swap_y(blocks[2]), swap_xy(blocks[3])]


def hidden_shard(weights, batch):
    places = [
        jnp.concatenate([w[:, a * (w.shape[1] // 4) : (a + 1) * (w.shape[1] // 4)] for w in weights], axis=1)
        for a in range(4)
    ]
    return jnp.concatenate(by_place(exchange(by_place(places, batch)), batch), axis=0)


def hidden_weights(weights, batch):
    return lax.all_gather(hidden_shard(weights, batch), "seq", axis=0, tiled=True)


def grad_shard(grad, batch):
    part = lax.psum_scatter(grad.astype(LOW), "seq", scatter_dimension=0, tiled=True)
    rows = part.shape[0] // 4
    places = [part[a * rows : (a + 1) * rows] for a in range(4)]
    return by_place(exchange(by_place(places, batch)), batch)


def columns_of(blocks, first, size):
    return jnp.concatenate([v[:, first : first + size] for v in blocks], axis=1).astype(jnp.float32)


def gather_rows(own, other):
    x_own, y_own = swap_x(own), swap_y(own)
    half = own.shape[0] // 2
    d_first = swap_y(x_own[:half])
    d_last = swap_x(y_own[half:])
    d_own = jnp.concatenate([d_first, d_last], axis=0)
    other = swap_core(own) if other is None else other
    groups = [(own, other)] + [(v, swap_core(v)) for v in (x_own, y_own, d_own)]
    return groups


def scatter_rows(make):
    sums = {}
    for group in (3, 1, 2, 0):
        away = swap_core(make(group, 1).astype(LOW))
        sums[group] = make(group, 0) + away.astype(jnp.float32)
    half = sums[3].shape[0] // 2
    diag = sums[3].astype(LOW)
    by_x = swap_x(diag[:half]).astype(jnp.float32)
    by_y = swap_y(diag[half:]).astype(jnp.float32)
    to_x = jnp.concatenate([sums[1][:half], sums[1][half:] + by_y], axis=0).astype(LOW)
    to_y = jnp.concatenate([sums[2][:half] + by_x, sums[2][half:]], axis=0).astype(LOW)
    return sums[0] + swap_x(to_x).astype(jnp.float32) + swap_y(to_y).astype(jnp.float32)


def sum_tokens(v):
    v = v.reshape(4, 2, -1)
    got = swap_core(v)
    v = v + jnp.stack([got[:, 1], got[:, 0]], axis=1)
    got = swap_x(v)
    v = v + jnp.stack([got[1], got[0], got[3], got[2]], axis=0)
    got = swap_y(v)
    v = v + jnp.stack([got[2], got[3], got[0], got[1]], axis=0)
    return v.reshape(8, -1)


def gather_tokens(v):
    v = jnp.stack([v, swap_core(v)])
    v = jnp.concatenate([v, swap_x(v)])
    return jnp.concatenate([v, swap_y(v)])


def sum_all(v, count):
    v = v + swap_x(v)
    v = v + swap_y(v)
    step = 1
    while step < count:
        v = v + lax.ppermute(v, "seq", [(i, i ^ step) for i in range(count)])
        step *= 2
    return v


def forward_kernel(seg, rows, decay_ref, input_ref, state_ref, product_ref):
    def body(t, carry):
        h, p = carry
        at = pl.ds(t, rows, stride=seg)
        d = decay_ref[at, :]
        h = d * h + input_ref[at, :]
        p = d * p
        state_ref[at, :] = h
        product_ref[at, :] = p
        return h, p

    first = pl.ds(0, rows, stride=seg)
    h, p = input_ref[first, :], decay_ref[first, :]
    state_ref[first, :] = h
    product_ref[first, :] = p
    lax.fori_loop(1, seg, body, (h, p), unroll=5)


def backward_kernel(seg, rows, decay_ref, input_ref, state_ref, product_ref):
    def body(k, carry):
        h, p, d = carry
        at = pl.ds(seg - 1 - k, rows, stride=seg)
        h = d * h + input_ref[at, :]
        p = d * p
        state_ref[at, :] = h
        product_ref[at, :] = p
        return h, p, decay_ref[at, :]

    last = pl.ds(seg - 1, rows, stride=seg)
    h, p = input_ref[last, :], decay_ref[last, :]
    state_ref[last, :] = h
    product_ref[last, :] = jnp.ones_like(p)
    at = pl.ds(seg - 2, rows, stride=seg)
    h = p * h + input_ref[at, :]
    state_ref[at, :] = h
    product_ref[at, :] = p
    lax.fori_loop(2, seg, body, (h, p, decay_ref[at, :]), unroll=2)


def scan_rows(kernel, decay, values, seg):
    count, width = decay.shape
    block = pl.BlockSpec((count, 128), lambda i: (0, i))
    return pl.pallas_call(
        functools.partial(kernel, seg, count // seg),
        grid=(width // 128,),
        in_specs=[block, block],
        out_specs=[block, block],
        out_shape=[jax.ShapeDtypeStruct((count, width), jnp.float32)] * 2,
        compiler_params=pltpu.CompilerParams(vmem_limit_bytes=32 * 1024 * 1024),
        cost_estimate=pl.CostEstimate(
            flops=3 * count * width, bytes_accessed=16 * count * width, transcendentals=0
        ),
    )(decay, values)


def enter(product, last, count, back):
    pair = jnp.stack([product, last])
    value = jnp.zeros_like(last)
    got = []
    for k in range(1, count):
        hops = [(i, i + k) for i in range(count - k)]
        if back:
            hops = [(b, a) for a, b in hops]
        got.append(lax.ppermute(pair, "seq", hops))
    for part in reversed(got):
        value = part[0] * value + part[1]
    return value


def shards(
    tokens_in,
    grad_out,
    w_input,
    w_forget,
    w_outgate,
    w_out,
    mlp_gate,
    mlp_up,
    mlp_down,
    gain_mixer,
    gain_mlp,
    gain_state,
    bound_param,
    layer_index,
    doc_lengths,
):
    rows, seg, width = tokens_in.shape
    half = gain_state.shape[0]
    chan = half // 4
    unit = mlp_gate.shape[1] // 4
    segments = lax.axis_size("seq")
    core = lax.axis_index("mp")
    batch = lax.axis_index("batch")
    place = lax.axis_index("seq")

    w_scan = hidden_weights((w_input, w_forget), batch)
    w_gates = hidden_weights((w_outgate, w_out.T), batch)
    w_mlp = hidden_weights((mlp_gate, mlp_up), batch)
    w_down = hidden_weights((mlp_down.T,), batch)
    w_gate, w_mix = w_gates[:, :chan], w_gates[:, chan:]

    own_table = lax.dynamic_slice_in_dim(bound_param, batch * chan, chan, 1)
    layers = bound_param.shape[0]
    layer = jnp.arange(layers, dtype=jnp.int32)[:, None]
    used = jnp.logical_and(layer >= 1, layer <= layer_index[0]).astype(jnp.float32)
    bound = jnp.sum(jax.nn.softmax(own_table, axis=0) * used, axis=0)
    lengths = jnp.where(core == 0, doc_lengths, doc_lengths[::-1])
    lengths = jnp.concatenate([lengths, swap_x(lengths), swap_y(lengths), swap_xy(lengths)])
    starts = jnp.cumsum(lengths, axis=1) - lengths
    places = place * seg + jnp.arange(seg, dtype=jnp.int32)
    resets = jnp.any(places[None, :, None] == starts[:, None, :], axis=2).astype(jnp.float32)
    keep_mask = (1.0 - resets).reshape(8 * seg, 1)

    gain_one = gain_mixer.astype(jnp.float32)
    gain_two = gain_mlp.astype(jnp.float32)
    gain_three = lax.dynamic_slice_in_dim(gain_state, batch * chan, chan, 0).astype(jnp.float32)

    def own_other(v):
        return (
            lax.dynamic_index_in_dim(v, core, 0, keepdims=False),
            lax.dynamic_index_in_dim(v, 1 - core, 0, keepdims=False),
        )

    tok_own, tok_other = own_other(tokens_in)
    cot_own, cot_other = own_other(grad_out)
    tok_own = tok_own.astype(jnp.float32)

    def normed(v, gain):
        inverse = lax.rsqrt(jnp.mean(v * v, axis=-1, keepdims=True) + EPSILON)
        return (v * inverse * gain).astype(LOW), inverse

    normed_own, inv_one = normed(tok_own, gain_one)
    normed_other, _ = normed(tok_other.astype(jnp.float32), gain_one)
    normed_in = jnp.concatenate(
        [v for group in gather_rows(normed_own, normed_other) for v in group], axis=0
    )
    cot_all = jnp.concatenate([v for group in gather_rows(cot_own, cot_other) for v in group], axis=0)

    proj_scan = plain_dot(normed_in, w_scan)
    proj_in, proj_forget = proj_scan[:, :chan], proj_scan[:, chan:]
    proj_gate = plain_dot(normed_in, w_gate)
    sig_forget = jax.nn.sigmoid(proj_forget)
    forget = bound + (1.0 - bound) * sig_forget
    sig_in = jax.nn.sigmoid(proj_in)
    act_in = proj_in * sig_in
    inputs = act_in * (1.0 - forget)
    decay = forget * keep_mask
    local_state, cum_decay = scan_rows(forward_kernel, decay, inputs, seg)

    def by_row(v):
        return v.reshape(8, seg, chan)

    carry_in = enter(by_row(cum_decay)[:, -1], by_row(local_state)[:, -1], segments, False)
    state = by_row(local_state) + by_row(cum_decay) * carry_in[:, None, :]
    previous = jnp.concatenate([carry_in[:, None, :], state[:, :-1]], axis=1).reshape(8 * seg, chan)
    square_total = sum_tokens(jnp.sum(state * state, axis=-1))
    inv_all = lax.rsqrt(square_total / width + EPSILON)
    inv_own = inv_all[0][:, None]
    inv_state = inv_all.reshape(8 * seg, 1)
    state = state.reshape(8 * seg, chan)
    sig_gate = jax.nn.sigmoid(proj_gate)
    act_gate = proj_gate * sig_gate
    gated_raw = (state * gain_three * act_gate).astype(LOW)

    def row_of(v, group, part):
        first = (2 * group + part) * seg
        return v[first : first + seg]

    mix_raw = scatter_rows(lambda g, p: right_dot(row_of(gated_raw, g, p), w_mix))
    resid = tok_own + inv_own * mix_raw

    normed_mlp_own, inv_two = normed(resid, gain_two)
    normed_mlp = jnp.concatenate(
        [v for group in gather_rows(normed_mlp_own, None) for v in group], axis=0
    )
    acts = plain_dot(normed_mlp, w_mlp)
    gate_act, up_act = acts[:, :unit], acts[:, unit:]
    sig_act = jax.nn.sigmoid(gate_act)
    silu_act = gate_act * sig_act
    hidden = (silu_act * up_act).astype(LOW)
    grad_down = grad_shard(left_dot(cot_all, hidden), batch)
    d_hidden = plain_dot(cot_all, w_down)
    d_gate = (d_hidden * up_act * sig_act * (1.0 + gate_act * (1.0 - sig_act))).astype(LOW)
    d_up = (d_hidden * silu_act).astype(LOW)
    d_acts = jnp.concatenate([d_gate, d_up], axis=1)
    d_normed_mlp = scatter_rows(lambda g, p: right_dot(row_of(d_acts, g, p), w_mlp))
    grad_mlp = grad_shard(left_dot(normed_mlp, d_acts), batch)
    mlp_own = scatter_rows(lambda g, p: right_dot(row_of(hidden, g, p), w_down))
    out_own = (resid + mlp_own).astype(LOW)

    gain_two_full = jnp.sum(d_normed_mlp * resid * inv_two, axis=0)
    d_resid = cot_own.astype(jnp.float32) + norm_back(d_normed_mlp, resid, gain_two, inv_two)
    d_resid_low = d_resid.astype(LOW)
    dot_own = jnp.sum(d_resid_low.astype(jnp.float32) * mix_raw, axis=-1)
    dot_total = gather_tokens(dot_own).reshape(8 * seg, 1)
    d_resid_all = jnp.concatenate(
        [v for group in gather_rows(d_resid_low, None) for v in group], axis=0
    )
    d_gated = plain_dot(d_resid_all, w_mix)
    state_normed = state * inv_state
    gated = (state_normed * gain_three * act_gate).astype(LOW)
    grad_mix = left_dot(d_resid_all, gated)
    gain_three_grad = jnp.sum(d_gated * state_normed * act_gate, axis=0)
    d_proj_gate = (
        d_gated * state_normed * gain_three * sig_gate * (1.0 + proj_gate * (1.0 - sig_gate))
    ).astype(LOW)
    d_normed_state = d_gated * gain_three * act_gate
    d_state = inv_state * d_normed_state - state * inv_state**3 * (dot_total / width)
    back_local, back_prod = scan_rows(backward_kernel, decay, d_state, seg)
    first_decay = by_row(decay)[:, 0]
    returned = enter(
        first_decay * by_row(back_prod)[:, 0],
        first_decay * by_row(back_local)[:, 0],
        segments,
        True,
    )
    lam = (by_row(back_local) + by_row(back_prod) * returned[:, None, :]).reshape(8 * seg, chan)
    d_forget = lam * (previous * keep_mask - act_in)
    d_proj_in = (lam * (1.0 - forget) * sig_in * (1.0 + proj_in * (1.0 - sig_in))).astype(LOW)
    d_proj_forget = (d_forget * (1.0 - bound) * sig_forget * (1.0 - sig_forget)).astype(LOW)
    bound_grad = jnp.sum(d_forget * (1.0 - sig_forget), axis=0)
    d_scan = jnp.concatenate([d_proj_in, d_proj_forget], axis=1)
    grad_gates = grad_shard(
        jnp.concatenate([left_dot(normed_in, d_proj_gate), grad_mix], axis=1), batch
    )
    grad_scan = grad_shard(left_dot(normed_in, d_scan), batch)
    d_normed_in = scatter_rows(
        lambda g, p: right_dot(row_of(d_scan, g, p), w_scan)
        + right_dot(row_of(d_proj_gate, g, p), w_gate)
    )
    gain_one_full = jnp.sum(d_normed_in * tok_own * inv_one, axis=0)
    grad_own = d_resid + norm_back(d_normed_in, tok_own, gain_one, inv_one)

    def both_rows(mine, got):
        return jnp.where(core == 0, jnp.stack([mine, got]), jnp.stack([got, mine]))

    out_halves = jnp.stack([out_own[:, :half], out_own[:, half:]])
    out_keep, out_send = own_other(out_halves)
    tokens_out = both_rows(out_keep, swap_core(out_send))
    grad_tokens = both_rows(grad_own, swap_core(grad_own))

    gains = jnp.stack([gain_one_full, gain_two_full]).reshape(2, 2, half)
    gains_keep = lax.dynamic_index_in_dim(gains, core, 1, keepdims=False)
    gains_send = lax.dynamic_index_in_dim(gains, 1 - core, 1, keepdims=False)
    channels = lax.dynamic_update_slice_in_dim(
        jnp.zeros((2, half), jnp.float32),
        jnp.stack([gain_three_grad, bound_grad]),
        batch * chan,
        1,
    )
    small = sum_all(jnp.concatenate([gains_keep + swap_core(gains_send), channels]), segments)
    soft = jax.nn.softmax(bound_param, axis=0)
    grad_table = small[3] * soft * (used - jnp.sum(soft * used, axis=0))
    return (
        tokens_out,
        grad_tokens,
        columns_of(grad_scan, 0, chan),
        columns_of(grad_scan, chan, chan),
        columns_of(grad_gates, 0, chan),
        columns_of(grad_gates, chan, chan).T,
        columns_of(grad_mlp, 0, unit),
        columns_of(grad_mlp, unit, unit),
        columns_of(grad_down, 0, unit).T,
        small[0],
        small[1],
        small[2],
        grad_table,
    )


def solution(mesh):
    return jax.shard_map(
        shards,
        mesh=mesh,
        in_specs=(
            P("batch", "seq", None),
            P("batch", "seq", None),
            P(("seq", "batch"), "mp"),
            P(("seq", "batch"), "mp"),
            P(("seq", "batch"), "mp"),
            P("mp", ("seq", "batch")),
            P(("seq", "batch"), "mp"),
            P(("seq", "batch"), "mp"),
            P("mp", ("seq", "batch")),
            P(),
            P(),
            P("mp"),
            P(None, "mp"),
            P(),
            P("batch", None),
        ),
        out_specs=(
            P("batch", "seq", "mp"),
            P("batch", "seq", None),
            P(("seq", "batch"), "mp"),
            P(("seq", "batch"), "mp"),
            P(("seq", "batch"), "mp"),
            P("mp", ("seq", "batch")),
            P(("seq", "batch"), "mp"),
            P(("seq", "batch"), "mp"),
            P("mp", ("seq", "batch")),
            P("mp"),
            P("mp"),
            P("mp"),
            P(None, "mp"),
        ),
        check_vma=False,
    )
```

```python
import functools

import jax
import jax.numpy as jnp
from jax import lax
from jax.experimental import pallas as pl
from jax.experimental.pallas import tpu as pltpu
from jax.sharding import PartitionSpec as P

EPSILON = 1e-06
LOW = jnp.bfloat16
FULL = jnp.float32
VMEM_BYTES = 56 * 1024 * 1024
ANYWHERE = pl.BlockSpec(memory_space=pl.ANY)


def swap_x(v):
    return lax.ppermute(v, "batch", [(i, i ^ 1) for i in range(4)])


def swap_y(v):
    return lax.ppermute(v, "batch", [(i, i ^ 2) for i in range(4)])


def swap_xy(v):
    return lax.ppermute(v, "batch", [(i, i ^ 3) for i in range(4)])


def swap_core(v):
    return lax.ppermute(v, "mp", [(0, 1), (1, 0)])


def after(v, *first):
    return lax.optimization_barrier((v, *first))[0]


def settled(*first):
    return swap_core(lax.optimization_barrier(first)[0][:16, :128])


def contract(left, right, left_dim, right_dim):
    return lax.dot_general(
        left, right, (((left_dim,), (right_dim,)), ((), ())), preferred_element_type=FULL
    )


def by_place(blocks, batch):
    stacked = jnp.stack(blocks)
    return [
        lax.dynamic_index_in_dim(stacked, jnp.bitwise_xor(batch, a), 0, keepdims=False)
        for a in range(4)
    ]


def exchange(blocks):
    return [blocks[0], swap_x(blocks[1]), swap_y(blocks[2]), swap_xy(blocks[3])]


def hidden_blocks(weights, batch):
    places = [
        jnp.concatenate(
            [w[:, a * (w.shape[1] // 4) : (a + 1) * (w.shape[1] // 4)] for w in weights], axis=1
        )
        for a in range(4)
    ]
    return lax.optimization_barrier(exchange(by_place(places, batch)))


def gather_width(shard):
    return lax.all_gather(shard, "seq", axis=0, tiled=True)


def shard_of(blocks, batch):
    return jnp.concatenate(by_place(blocks, batch), axis=0)


def scatter_width(grad):
    return lax.psum_scatter(grad, "seq", scatter_dimension=0, tiled=True)


def rows_by_place(part, batch):
    rows = part.shape[0] // 4
    return by_place([part[a * rows : (a + 1) * rows] for a in range(4)], batch)


def gather_rows(own, then=(), between=()):
    first, last = own
    late_first, late_last = lax.optimization_barrier((first, last, *between))[:2]
    x_first, y_last, x_last, y_first = lax.optimization_barrier(
        (swap_x(first), swap_y(last), swap_x(late_last), swap_y(late_first), *then)
    )[:4]
    d_first, d_last = lax.optimization_barrier((swap_y(x_first), swap_x(y_last)))
    return [first, last, x_first, x_last, y_first, y_last, d_first, d_last]


def scatter_rows(terms, then=()):
    mine, x_first, x_last, y_first, y_last, d_first, d_last = terms
    by_x, by_y, gx_first, gy_last = lax.optimization_barrier(
        (swap_x(d_first), swap_y(d_last), swap_x(x_first), swap_y(y_last), *then)
    )[:4]
    x_last = (x_last + by_y.astype(FULL)).astype(LOW)
    y_first = (y_first + by_x.astype(FULL)).astype(LOW)
    gx_last, gy_first = lax.optimization_barrier((swap_x(x_last), swap_y(y_first)))
    return [mine, gx_first, gx_last, gy_first, gy_last], (x_last, y_first)


def sum_tokens(v):
    got = swap_x(v)
    v = v + jnp.stack([got[1], got[0], got[3], got[2]])
    got = swap_y(v)
    return v + jnp.stack([got[2], got[3], got[0], got[1]])


def sum_all(v, count):
    v = v + swap_x(v)
    v = v + swap_y(v)
    step = 1
    while step < count:
        v = v + lax.ppermute(v, "seq", [(i, i ^ step) for i in range(count)])
        step *= 2
    return v


def enter(product, last, count, back):
    def shift(pair, k):
        hops = [(i, i + k) for i in range(count - k)]
        return lax.ppermute(pair, "seq", [(b, a) for a, b in hops] if back else hops)

    def link(earlier, later):
        return jnp.stack([earlier[0] * later[0], later[0] * earlier[1] + later[1]])

    ends = jnp.stack([product, last])
    value = shift(ends, 1)
    step = 2
    while step < count:
        value = link(shift(link(value, ends), step), value)
        step *= 2
    return value[1]


def call(kernel, arrays, outs, scratch, cost, first=()):
    count = len(arrays)
    arrays = [*arrays, *first]

    def body(*refs):
        kernel(*refs[:count], *refs[len(arrays) :])

    return pl.pallas_call(
        body,
        in_specs=[ANYWHERE] * len(arrays),
        out_specs=[ANYWHERE] * len(outs),
        out_shape=[jax.ShapeDtypeStruct(shape, kind) for shape, kind in outs],
        scratch_shapes=[
            pltpu.SemaphoreType.DMA(v) if isinstance(v[0], int) else pltpu.VMEM(*v) for v in scratch
        ],
        compiler_params=pltpu.CompilerParams(vmem_limit_bytes=VMEM_BYTES),
        cost_estimate=pl.CostEstimate(
            flops=0, bytes_accessed=int(cost * 3.5e6), transcendentals=0
        ),
    )(*arrays)


def copy_in(source, target, sem):
    copy = pltpu.make_async_copy(source, target, sem)
    copy.start()
    return copy


def wait_all(copies):
    for copy in copies:
        copy.wait()


def dot_kernel(n, first, wide, *refs):
    xs, ws, out, (x_s, w_s, o_s, x_sem, w_sem, out_sem) = (
        refs[: 2 * n],
        refs[2 * n : 2 * n + 2],
        refs[2 * n + 2],
        refs[2 * n + 3 :],
    )
    rows = x_s.shape[1] // 2
    cols = pl.ds(first, wide)
    loads_w = [copy_in(ws[0].at[:, cols], w_s.at[0], w_sem.at[0])]
    loads = []
    for p, x in enumerate(xs):
        x = x.at[:, pl.ds(0, x_s.shape[2])]
        loads.append(copy_in(x, x_s.at[p // 2, pl.ds(p % 2 * rows, rows)], x_sem.at[p]))
        if p == 1:
            loads_w.append(copy_in(ws[1].at[:, cols], w_s.at[1], w_sem.at[1]))
    stores = []
    for r in range(n):
        wait_all(loads[2 * r : 2 * r + 2])
        for h in range(2):
            if r == 0:
                loads_w[h].wait()
            o_s[2 * r + h] = contract(x_s[r], w_s[h], 1, 0)
            at = pl.ds((2 * r + h) * 2 * rows, 2 * rows)
            stores.append(copy_in(o_s.at[2 * r + h], out.at[at], out_sem.at[2 * r + h]))
    wait_all(stores)


def rows_dot(xs, ws, first, wide, cost=7):
    n, rows, depth = len(xs) // 2, xs[0].shape[0], ws[0].shape[0]
    return call(
        functools.partial(dot_kernel, n, first, wide),
        [*xs, *ws],
        [((4 * n * rows, wide), FULL)],
        [
            ((n, 2 * rows, depth), LOW),
            ((2, depth, wide), LOW),
            ((2 * n, 2 * rows, wide), FULL),
            (2 * n,),
            (2,),
            (2 * n,),
        ],
        cost,
    )[0]


def acts_kernel(n, *refs):
    xs, w, outs, held, (x_s, w_s, sem, out_sem) = (
        refs[: 2 * n],
        refs[2 * n],
        refs[2 * n + 1 : 2 * n + 4],
        refs[2 * n + 4 : 2 * n + 7],
        refs[2 * n + 7 :],
    )
    rows, unit = x_s.shape[1] // 2, held[0].shape[1]
    load_w = copy_in(w, w_s, sem.at[2 * n])
    loads = [
        copy_in(x, x_s.at[p // 2, pl.ds(p % 2 * rows, rows)], sem.at[p]) for p, x in enumerate(xs)
    ]
    load_w.wait()
    stores = []
    for r in range(n):
        wait_all(loads[2 * r : 2 * r + 2])
        acts = contract(x_s[r], w_s[...], 1, 0)
        g, u = acts[:, :unit], acts[:, unit:]
        at = pl.ds(r * 2 * rows, 2 * rows)
        held[0][at, :] = g
        held[1][at, :] = u
        held[2][at, :unit] = (g * jax.nn.sigmoid(g) * u).astype(LOW)
        held[2][at, unit:] = jnp.zeros((2 * rows, held[2].shape[1] - unit), LOW)
        for k in range(3):
            stores.append(copy_in(held[k].at[at], outs[k].at[at], out_sem.at[r, k]))
    wait_all(stores)


def rows_acts(xs, w):
    n, (rows, depth), unit = len(xs) // 2, xs[0].shape, w.shape[1] // 2
    padded = pl.cdiv(unit, 128) * 128
    outs = [((2 * n * rows, v), kind) for v, kind in ((unit, FULL), (unit, FULL), (padded, LOW))]
    return call(
        functools.partial(acts_kernel, n),
        [*xs, w],
        outs,
        [*outs, ((n, 2 * rows, depth), LOW), (w.shape, LOW), (2 * n + 1,), (n, 3)],
        12,
    )


def grad_kernel(x_at, y_at, more, *refs):
    n = len(y_at)
    outs, (x_s, y_s, m_s), held = refs[-5 - 2 * n - 2 : -5 - n - 2], refs[-5 - n - 2 : -4 - n], refs[-4 - n : -4]
    x_sem, y_sem, m_sem, out_sem = refs[-4:]
    wide = held[0].shape[1]
    chunks = [chunk for group in y_at for chunk in group]
    each = y_s.shape[1] // len(chunks)
    loads = []
    for g, (target, places) in enumerate(((x_s, x_at), *[(y_s, v) for v in chunks])):
        start = 0
        for k, (i, first, rows) in enumerate(places):
            at = target.at[pl.ds(start, rows)]
            if g:
                at = target.at[pl.ds(start, rows), pl.ds((g - 1) * each, each)]
            sem = y_sem.at[g - 1, k] if g else x_sem.at[k]
            source = refs[i].at[pl.ds(first, rows), pl.ds(0, at.shape[1])]
            loads.append(copy_in(source, at, sem))
            start += rows
    if more is not None:
        load_more = copy_in(refs[more], m_s, m_sem.at[0])
    wait_all(loads)
    depth, stores = x_s.shape[1], []
    for block, first in enumerate(range(0, depth, 256)):
        cols = pl.ds(first, min(256, depth - first))
        total = contract(x_s[:, cols], y_s[...], 0, 0)
        if more is not None:
            if block == 0:
                load_more.wait()
            total = total + m_s[cols, :].astype(FULL)
        for g in range(n):
            held[g][cols, :] = total[:, g * wide : (g + 1) * wide].astype(LOW)
            stores.append(copy_in(held[g].at[cols], outs[g].at[cols], out_sem.at[g, block]))
    wait_all(stores)


def rows_grad(xs, groups, cost, more=None, depth=None):
    arrays, x_at, y_at = list(xs), [(k, 0, x.shape[0]) for k, x in enumerate(xs)], []
    for group in groups:
        y_at.append([])
        for chunk in group:
            y_at[-1].append([])
            for v, first, rows in chunk:
                found = [k for k, other in enumerate(arrays) if other is v]
                if not found:
                    found = [len(arrays)]
                    arrays.append(v)
                y_at[-1][-1].append((found[0], first, rows))
    count = sum(rows for _, _, rows in x_at)
    depth = depth or xs[0].shape[1]
    n, each = len(groups), groups[0][0][0][0].shape[1]
    wide = each * len(groups[0])
    at = None
    if more is not None:
        at = len(arrays)
        arrays.append(more)
    outs = [((depth, wide), LOW)] * n
    return call(
        functools.partial(grad_kernel, x_at, y_at, at),
        arrays,
        outs,
        [
            ((count, depth), LOW),
            ((count, n * wide), LOW),
            ((depth if more is not None else 16, wide), LOW),
            *outs,
            (len(x_at),),
            (n * len(groups[0]), len(y_at[0][0])),
            (1,),
            (n, pl.cdiv(depth, 256)),
        ],
        cost,
    )


def block_pieces(v, half, seg):
    return [(v, (2 * r + half) * seg, seg) for r in range(4)]


PIECES = (((0, 2, FULL),), ((0, 1, LOW), (1, 2, FULL)), ((0, 1, FULL), (1, 2, LOW)), ((0, 1, LOW), (1, 2, LOW)))


def term_outs(picked, seg, wide):
    return [
        (((b - a) * seg // 2, wide), kind) for r in picked for a, b, kind in PIECES[r]
    ]


def store_term(term, r, seg, held, outs, sem, start):
    stores = []
    for k, (a, b, kind) in enumerate(PIECES[r]):
        held[start + k][...] = term[a * seg // 2 : b * seg // 2].astype(kind)
        stores.append(copy_in(held[start + k], outs[start + k], sem.at[start + k]))
    return stores


def term_kernel(picked, parts, count, *refs):
    n = sum(len(PIECES[r]) for r in picked)
    arrays, outs, held = refs[:count], refs[count : count + n], refs[count + n : count + 2 * n]
    scratch = refs[count + 2 * n :]
    l_s, w_s = scratch[: len(parts)], scratch[len(parts) : 2 * len(parts)]
    l_sem, w_sem, out_sem = scratch[2 * len(parts) :]
    seg = l_s[0].shape[1]
    loads, loads_w = [], []
    for k, r in enumerate(picked):
        loads.append([])
        for p, (left, (each, half), w, first, depth) in enumerate(parts):
            if k == 0:
                source = arrays[w].at[:, pl.ds(first, depth)]
                loads_w.append(copy_in(source, w_s[p], w_sem.at[p]))
            at = pl.ds((each * r + half) * seg, seg)
            loads[k].append(copy_in(arrays[left].at[at], l_s[p].at[k], l_sem.at[k, p]))
    stores, start = [], 0
    for k, r in enumerate(picked):
        term = None
        for p in range(len(parts)):
            loads[k][p].wait()
            if k == 0:
                loads_w[p].wait()
            part = contract(l_s[p][k], w_s[p][...], 1, 1)
            term = part if term is None else term + part
        stores += store_term(term, r, seg, held, outs, out_sem, start)
        start += len(PIECES[r])
    wait_all(stores)


def rows_terms(parts, picked, seg, first=(), cost=0):
    arrays, places = [], []
    for left, block, w, column in parts:
        at = []
        for v in (left, w):
            found = [k for k, other in enumerate(arrays) if other is v]
            if not found:
                found = [len(arrays)]
                arrays.append(v)
            at.append(found[0])
        places.append((at[0], block, at[1], column, left.shape[1]))
    wide = parts[0][2].shape[0]
    outs = term_outs(picked, seg, wide)
    return call(
        functools.partial(term_kernel, picked, places, len(arrays)),
        arrays,
        outs,
        [
            *outs,
            *[((len(picked), seg, depth), LOW) for *_, depth in places],
            *[((wide, depth), LOW) for *_, depth in places],
            (len(picked), len(parts)),
            (len(parts),),
            (len(outs),),
        ],
        cost,
        first,
    )


def back_kernel(picked, *refs):
    n = len(picked)
    m = sum(len(PIECES[r]) for r in picked)
    dys, gates, ups, downs, mlps, d_acts = (
        refs[: 2 * n],
        refs[2 * n : 2 * n + 2],
        refs[2 * n + 2 : 2 * n + 4],
        refs[2 * n + 4 : 2 * n + 6],
        refs[2 * n + 6 : 2 * n + 8],
        refs[2 * n + 8],
    )
    outs, held = refs[2 * n + 9 : 2 * n + 9 + m], refs[2 * n + 9 + m : 2 * n + 9 + 2 * m]
    y_s, g_s, u_s, down_s, mlp_s, a_s, y_sem, act_sem, w_sem, a_sem, out_sem = refs[
        2 * n + 9 + 2 * m :
    ]
    seg, unit = g_s.shape[2:]
    loads_w, loads_y, loads_act = [], [], []
    for k, r in enumerate(picked):
        at = pl.ds(r * seg, seg)
        loads_y.append(
            [
                copy_in(
                    dys[2 * k + p], y_s.at[k, pl.ds(p * seg // 2, seg // 2)], y_sem.at[k, p]
                )
                for p in range(2)
            ]
        )
        loads_act.append([])
        for h in range(2):
            if k == 0:
                loads_w.append(copy_in(downs[h], down_s.at[h], w_sem.at[h, 0]))
            loads_act[k].append(
                [
                    copy_in(gates[h].at[at], g_s.at[k, h], act_sem.at[k, h, 0]),
                    copy_in(ups[h].at[at], u_s.at[k, h], act_sem.at[k, h, 1]),
                ]
            )
            if k == 0:
                loads_w.append(copy_in(mlps[h], mlp_s.at[h], w_sem.at[h, 1]))
    stores, start = [], 0
    for k, r in enumerate(picked):
        wait_all(loads_y[k])
        term = None
        for h in range(2):
            if k == 0:
                loads_w[2 * h].wait()
            d_hidden = contract(y_s[k], down_s[h], 1, 0)[:, :unit]
            wait_all(loads_act[k][h])
            g, u = g_s[k, h], u_s[k, h]
            sig = jax.nn.sigmoid(g)
            a_s[k, h, :, :unit] = (d_hidden * u * sig * (1.0 + g * (1.0 - sig))).astype(LOW)
            a_s[k, h, :, unit:] = (d_hidden * (g * sig)).astype(LOW)
            at = pl.ds((2 * k + h) * seg, seg)
            stores.append(copy_in(a_s.at[k, h], d_acts.at[at], a_sem.at[k, h]))
            if k == 0:
                loads_w[2 * h + 1].wait()
            part = contract(a_s[k, h], mlp_s[h], 1, 1)
            term = part if term is None else term + part
        stores += store_term(term, r, seg, held, outs, out_sem, start)
        start += len(PIECES[r])
    wait_all(stores)


def rows_back(dys, gates, ups, downs, mlps, picked, seg, cost):
    n, (wide, both) = len(picked), mlps[0].shape
    unit = both // 2
    outs = term_outs(picked, seg, wide)
    return call(
        functools.partial(back_kernel, picked),
        [*[dys[2 * r + p] for r in picked for p in range(2)], *gates, *ups, *downs, *mlps],
        [((2 * n * seg, both), LOW), *outs],
        [
            *outs,
            ((n, seg, wide), LOW),
            ((n, 2, seg, unit), FULL),
            ((n, 2, seg, unit), FULL),
            ((2, *downs[0].shape), LOW),
            ((2, wide, both), LOW),
            ((n, 2, seg, both), LOW),
            (n, 2),
            (n, 2, 2),
            (2, 2),
            (n, 2),
            (len(outs),),
        ],
        cost,
    )


def channel_call(kernel, arrays, outs, scratch=(), cost=0):
    def spec(shape, skip=0):
        if shape[1] == 1:
            return pl.BlockSpec(shape, lambda i: (0, 0))
        return pl.BlockSpec((shape[0], 128), lambda i: (0, i + skip))

    skips = [v[1] if isinstance(v, tuple) else 0 for v in arrays]
    arrays = [v[0] if isinstance(v, tuple) else v for v in arrays]

    return pl.pallas_call(
        kernel,
        grid=(2,),
        in_specs=[spec(v.shape, skip) for v, skip in zip(arrays, skips)],
        out_specs=[spec(shape) for shape, _ in outs],
        out_shape=[jax.ShapeDtypeStruct(shape, kind) for shape, kind in outs],
        scratch_shapes=[pltpu.VMEM(*v) for v in scratch],
        compiler_params=pltpu.CompilerParams(vmem_limit_bytes=VMEM_BYTES),
        cost_estimate=pl.CostEstimate(
            flops=0, bytes_accessed=int(cost * 3.5e6), transcendentals=0
        ),
    )(*arrays)


def forward_scan(seg, rows, decay_ref, input_ref, state_ref, product_ref):
    def body(t, carry):
        h, p = carry
        at = pl.ds(t, rows, stride=seg)
        d = decay_ref[at, :]
        h = d * h + input_ref[at, :]
        p = d * p
        state_ref[at, :] = h
        product_ref[at, :] = p
        return h, p

    first = pl.ds(0, rows, stride=seg)
    h, p = input_ref[first, :], decay_ref[first, :]
    state_ref[first, :] = h
    product_ref[first, :] = p
    lax.fori_loop(1, seg, body, (h, p), unroll=5)


def backward_scan(seg, rows, decay_ref, input_ref, state_ref, product_ref):
    def body(k, carry):
        h, p, d = carry
        at = pl.ds(seg - 1 - k, rows, stride=seg)
        h = d * h + input_ref[at, :]
        p = d * p
        state_ref[at, :] = h
        product_ref[at, :] = p
        return h, p, decay_ref[at, :]

    last = pl.ds(seg - 1, rows, stride=seg)
    h, p = input_ref[last, :], decay_ref[last, :]
    state_ref[last, :] = h
    product_ref[last, :] = jnp.ones_like(p)
    at = pl.ds(seg - 2, rows, stride=seg)
    h = p * h + input_ref[at, :]
    state_ref[at, :] = h
    product_ref[at, :] = p
    lax.fori_loop(2, seg, body, (h, p, decay_ref[at, :]), unroll=2)


def scan_kernel(seg, proj_in, proj_forget, bound, keep, decay, local, product, inputs):
    rows = bound.shape[0]
    for k in range(rows):
        at = pl.ds(k * seg, seg)
        low = bound[pl.ds(k, 1), :]
        forget = low + (1.0 - low) * jax.nn.sigmoid(proj_forget[at, :])
        v = proj_in[at, :]
        decay[at, :] = forget * keep[at, :]
        inputs[at, :] = v * jax.nn.sigmoid(v) * (1.0 - forget)
    forward_scan(seg, rows, decay, inputs, local, product)


def state_kernel(seg, local, product, carry, gate, gain, state, gated, squares):
    first = pl.program_id(0) == 0
    for k in range(carry.shape[0]):
        at, one = pl.ds(k * seg, seg), pl.ds(k, 1)
        h = local[at, :] + product[at, :] * carry[one, :]
        g = gate[at, :]
        state[at, :] = h
        gated[at, :] = (h * gain[one, :] * (g * jax.nn.sigmoid(g))).astype(LOW)
        total = jnp.sum(h * h, axis=-1, keepdims=True)
        squares[at, :] = jnp.where(first, 0.0, squares[at, :]) + total


def gate_back_kernel(
    seg, wide, d_gated, gate, state, gain, inverse, dot, decay, gated, d_gate, gain_sum, local, product, held
):
    rows = gain.shape[0]
    for k in range(rows):
        at, one = pl.ds(k * seg, seg), pl.ds(k, 1)
        up, g, h, scale, inv = d_gated[at, :], gate[at, :], state[at, :], gain[one, :], inverse[at, :]
        sig = jax.nn.sigmoid(g)
        act, normed = g * sig, h * inv
        gated[at, :] = (normed * scale * act).astype(LOW)
        d_gate[at, :] = (up * normed * scale * sig * (1.0 + g * (1.0 - sig))).astype(LOW)
        gain_sum[one, :] = jnp.sum(up * normed * act, axis=0, keepdims=True)
        shrink = inv * inv * inv * (dot[at, :] * (1.0 / wide))
        held[at, :] = inv * (up * scale * act) - h * shrink
    backward_scan(seg, rows, decay, held, local, product)


def scan_back_kernel(
    seg, local, product, returned, state, carry, proj_in, proj_forget, bound, keep, d_in_ref, d_forget_ref, bound_sum
):
    for k in range(bound.shape[0]):
        at, one = pl.ds(k * seg, seg), pl.ds(k, 1)
        lam = local[at, :] + product[at, :] * returned[one, :]
        h = state[at, :]
        step = lax.broadcasted_iota(jnp.int32, h.shape, 0)
        previous = jnp.where(step == 0, carry[one, :], pltpu.roll(h, 1, 0))
        low, v = bound[one, :], proj_in[at, :]
        sig_forget, sig_in = jax.nn.sigmoid(proj_forget[at, :]), jax.nn.sigmoid(v)
        forget = low + (1.0 - low) * sig_forget
        d_forget = lam * (previous * keep[at, :] - v * sig_in)
        d_in = lam * (1.0 - forget) * sig_in * (1.0 + v * (1.0 - sig_in))
        d_in_ref[at, :] = d_in.astype(LOW)
        d_forget_ref[at, :] = (d_forget * (1.0 - low) * sig_forget * (1.0 - sig_forget)).astype(LOW)
        bound_sum[one, :] = jnp.sum(d_forget * (1.0 - sig_forget), axis=0, keepdims=True)


STEP = 32


def token_call(kernel, arrays, outs, seg, wide, cost=5):
    half = seg // 2

    def spec(shape):
        if shape[0] == 1:
            return pl.BlockSpec(shape, lambda i: (0, 0))
        if shape[0] == 2:
            return pl.BlockSpec((2, STEP, shape[2]), lambda i: (0, i, 0))
        return pl.BlockSpec((STEP, shape[1]), lambda i: (i, 0))

    def folded(shape):
        return (2, half, shape[1]) if shape[0] == seg else shape

    arrays = [v.reshape(folded(v.shape)) for v in arrays]
    got = pl.pallas_call(
        kernel,
        grid=(half // STEP,),
        in_specs=[spec(v.shape) for v in arrays],
        out_specs=[spec(folded(shape)) for shape, _ in outs],
        out_shape=[jax.ShapeDtypeStruct(folded(shape), kind) for shape, kind in outs],
        compiler_params=pltpu.CompilerParams(vmem_limit_bytes=VMEM_BYTES),
        cost_estimate=pl.CostEstimate(
            flops=0, bytes_accessed=int(cost * 3.5e6), transcendentals=0
        ),
    )(*arrays)
    return [v.reshape(shape) for v, (shape, _) in zip(got, outs)]


def both_rows(core, mine, got):
    return jnp.where(core == 0, jnp.stack([mine, got]), jnp.stack([got, mine]))


def final_kernel(place, core, *refs):
    mlp, mixer, (mine, got), refs = refs[:4], refs[4:8], refs[8:10], refs[10:]
    outs, (m_s, x_s, t_s), refs = refs[:8], refs[8:11], refs[11:]
    held, (sem, out_sem) = refs[:7], refs[7:]
    rows = [copy_in(v, t_s.at[k], sem.at[8 + k]) for k, v in enumerate((mine, got))]
    loads = [copy_in(v, m_s.at[k], sem.at[k]) for k, v in enumerate(mlp)]
    loads += [copy_in(v, x_s.at[k], sem.at[4 + k]) for k, v in enumerate(mixer)]
    wait_all(rows)
    stores = [
        copy_in(t_s.at[0], outs[7].at[core[0]], out_sem.at[7]),
        copy_in(t_s.at[1], outs[7].at[1 - core[0]], out_sem.at[8]),
    ]
    wait_all(loads)
    chan, unit = held[0].shape[1] // 4, held[4].shape[1] // 4
    for a in range(4):
        block = jnp.bitwise_xor(place[0], a)
        m, x = m_s[block].astype(FULL), x_s[block].astype(FULL)
        for k in range(3):
            held[k][:, a * chan : (a + 1) * chan] = x[:, k * chan : (k + 1) * chan]
        held[3][a * chan : (a + 1) * chan, :] = x[:, 3 * chan : 4 * chan].T
        for k in range(2):
            held[4 + k][:, a * unit : (a + 1) * unit] = m[:, k * unit : (k + 1) * unit]
        held[6][a * unit : (a + 1) * unit, :] = m[:, 2 * unit : 3 * unit].T
    stores += [copy_in(held[k], outs[k], out_sem.at[k]) for k in range(7)]
    wait_all(stores)


def final(place, core, mlp, mixer, mine, got, half, hidden, first):
    rows = mixer[0].shape[0]
    outs = [((rows, half), FULL)] * 3 + [((half, rows), FULL)]
    outs += [((rows, hidden), FULL)] * 2 + [((hidden, rows), FULL)]
    arrays = [*mlp, *mixer, mine, got, *first]
    more = [((2, *mine.shape), FULL)]

    def body(place_ref, core_ref, *refs):
        final_kernel(place_ref, core_ref, *refs[:10], *refs[len(arrays) :])

    return pl.pallas_call(
        body,
        in_specs=[pl.BlockSpec(memory_space=pltpu.SMEM)] * 2 + [ANYWHERE] * len(arrays),
        out_specs=[ANYWHERE] * 8,
        out_shape=[jax.ShapeDtypeStruct(shape, kind) for shape, kind in outs + more],
        scratch_shapes=[
            pltpu.VMEM((4, *mlp[0].shape), LOW),
            pltpu.VMEM((4, *mixer[0].shape), LOW),
            pltpu.VMEM((2, *mine.shape), FULL),
            *[pltpu.VMEM(*v) for v in outs],
            pltpu.SemaphoreType.DMA((10,)),
            pltpu.SemaphoreType.DMA((9,)),
        ],
        compiler_params=pltpu.CompilerParams(vmem_limit_bytes=VMEM_BYTES),
    )(place.reshape(1), core.reshape(1), *arrays)


def total_of(refs, h):
    mine, gx_first, gx_last, gy_first, gy_last = refs
    got_x, got_y = ((gx_first, gy_first), (gx_last, gy_last))[h]
    return mine[h] + got_x[...].astype(FULL) + got_y[...].astype(FULL)


def inverse_of(v):
    return lax.rsqrt(jnp.mean(v * v, axis=-1, keepdims=True) + EPSILON)


def enter_kernel(tok, gain, first, last, inverse):
    for h, out in enumerate((first, last)):
        v = tok[h].astype(FULL)
        inv = inverse_of(v)
        out[...] = (v * inv * gain[...]).astype(LOW)
        inverse[h] = inv


def mixed_kernel(*refs):
    *sums, tok, inv_state, gain, mix, resid, first, last, inverse = refs
    for h, out in enumerate((first, last)):
        raw = total_of(sums, h)
        v = tok[h].astype(FULL) + inv_state[h] * raw
        inv = inverse_of(v)
        mix[h] = raw
        resid[h] = v
        out[...] = (v * inv * gain[...]).astype(LOW)
        inverse[h] = inv


def norm_back(upstream, v, scale, inv):
    weighted = upstream * scale
    mean = jnp.mean(weighted * v, axis=-1, keepdims=True)
    return inv * weighted - v * (inv * inv * inv * mean)


def add_rows(ref, v):
    total = jnp.sum(v, axis=0, keepdims=True)

    @pl.when(pl.program_id(0) == 0)
    def _():
        ref[...] = jnp.zeros_like(ref)

    ref[...] += total


def d_mlp_kernel(*refs):
    *sums, resid, inverse, cot_first, cot_last, gain, mix, d_resid, first, last, gain_sum = refs
    terms = 0.0
    for h, (cot, out) in enumerate(((cot_first, first), (cot_last, last))):
        up, v, inv = total_of(sums, h), resid[h], inverse[h]
        terms = terms + up * v * inv
        grad = cot[...].astype(FULL) + norm_back(up, v, gain[...], inv)
        low = grad.astype(LOW)
        d_resid[h] = grad
        wide = low.shape[1]
        out[:, :wide] = low
        dot = jnp.sum(low.astype(FULL) * mix[h], axis=-1, keepdims=True)
        high = dot.astype(LOW)
        dot = dot - high.astype(FULL)
        middle = dot.astype(LOW)
        rest = (dot - middle.astype(FULL)).astype(LOW)
        lane = lax.broadcasted_iota(jnp.int32, (low.shape[0], 128), 1)
        parts = jnp.where(lane == 1, middle.astype(FULL), jnp.where(lane == 2, rest.astype(FULL), 0.0))
        out[:, wide:] = jnp.where(lane == 0, high.astype(FULL), parts).astype(LOW)
    add_rows(gain_sum, terms)


def d_in_kernel(*refs):
    *sums, tok, inverse, gain, d_resid, grad, gain_sum = refs
    terms = 0.0
    for h in range(2):
        up, v, inv = total_of(sums, h), tok[h].astype(FULL), inverse[h]
        terms = terms + up * v * inv
        grad[h] = d_resid[h] + norm_back(up, v, gain[...], inv)
    add_rows(gain_sum, terms)


def out_kernel(*refs):
    *sums, resid, out = refs
    for h in range(2):
        out[h] = (resid[h] + total_of(sums, h)).astype(LOW)


def shards(
    tokens_in,
    grad_out,
    w_input,
    w_forget,
    w_outgate,
    w_out,
    mlp_gate,
    mlp_up,
    mlp_down,
    gain_mixer,
    gain_mlp,
    gain_state,
    bound_param,
    layer_index,
    doc_lengths,
):
    rows, seg, width = tokens_in.shape
    half = gain_state.shape[0]
    chan = half // 4
    unit = mlp_gate.shape[1] // 4
    segments = lax.axis_size("seq")
    core = lax.axis_index("mp")
    batch = lax.axis_index("batch")
    place = lax.axis_index("seq")
    piece = (seg // 2, width)
    wider = (seg // 2, width + 128)
    whole = (seg, width)
    column = (seg, 1)

    def own_other(v):
        return [v, swap_core(v)]

    mixer = hidden_blocks((w_input, w_forget, w_outgate, w_out.T), batch)
    shard = shard_of(mixer, batch)
    w_scan, w_gates = gather_width(shard[:, : 2 * chan]), gather_width(shard[:, 2 * chan :])
    layers = bound_param.shape[0]
    layer = jnp.arange(layers, dtype=jnp.int32)[:, None]
    used = jnp.logical_and(layer >= 1, layer <= layer_index[0]).astype(FULL)
    table = jnp.concatenate([bound_param, gain_state.astype(FULL)[None]])
    table = jnp.stack(own_other(lax.dynamic_slice_in_dim(table, batch * chan, chan, 1)))
    bound = jnp.tile(jnp.sum(jax.nn.softmax(table[:, :layers], axis=1) * used, axis=1), (4, 1))
    gain_three = jnp.tile(table[:, layers], (4, 1))
    lengths = lax.dynamic_slice_in_dim(doc_lengths, core, 1, 0)
    lengths = jnp.concatenate([lengths, swap_x(lengths)])
    lengths = jnp.concatenate([lengths, swap_y(lengths)])
    starts = jnp.cumsum(lengths, axis=1) - lengths
    places = place * seg + jnp.arange(seg, dtype=jnp.int32)
    resets = jnp.any(places[None, :, None] == starts[:, None, :], axis=2).astype(FULL)
    keep_mask = jnp.repeat(1.0 - resets, 2, axis=0).reshape(8 * seg, 1)
    mlp_blocks = hidden_blocks((after(mlp_gate, lengths, table, *mixer), mlp_up, mlp_down.T), batch)
    shard = shard_of(mlp_blocks, batch)
    w_mlp, down = gather_width(shard[:, : 2 * unit]), shard[:, 2 * unit :]
    down = jnp.pad(down, ((0, 0), (0, -unit % 128)))

    gain_one = gain_mixer.astype(FULL)[None]
    gain_two = gain_mlp.astype(FULL)[None]
    tok_own, cot_own = lax.optimization_barrier(
        [lax.dynamic_index_in_dim(v, core, 0, keepdims=False) for v in (tokens_in, grad_out)]
    )

    def by_row(v):
        return v.reshape(8, seg, chan)

    def columns(v):
        return jnp.repeat(v, 2, axis=0).reshape(8 * seg, 1)

    channel = ((8 * seg, chan), FULL)

    *normed, inv_one = token_call(
        enter_kernel,
        [tok_own, gain_one],
        [(piece, LOW), (piece, LOW), (column, FULL)],
        seg,
        width,
    )
    normed = lax.optimization_barrier((*normed, *mixer))[:2]
    normed_in = gather_rows(normed, (), mlp_blocks)
    w_scan = own_other(after(w_scan, normed_in[6]))
    proj_scan = rows_dot(normed_in, w_scan, 0, 2 * chan, 0)
    proj_in, proj_forget = (proj_scan, 0), (proj_scan, chan // 128)
    decay, local_state, cum_decay = channel_call(
        functools.partial(scan_kernel, seg),
        [proj_in, proj_forget, bound, keep_mask],
        [channel] * 3,
        [((8 * seg, 128), FULL)],
    )
    w_gates = own_other(after(w_gates, local_state))
    carry_in = enter(by_row(cum_decay)[:, -1], by_row(local_state)[:, -1], segments, False)
    cot_pieces = [cot_own[: seg // 2], cot_own[seg // 2 :]]
    proj_gate = rows_dot(normed_in, w_gates, 0, chan, 0)
    carry_in = after(carry_in, proj_gate)
    state, gated_raw, squares = channel_call(
        functools.partial(state_kernel, seg),
        [local_state, cum_decay, carry_in, proj_gate, gain_three],
        [channel, ((8 * seg, chan), LOW), ((8 * seg, 1), FULL)],
    )
    square_total = sum_tokens(jnp.sum(squares.reshape(4, 2, seg), axis=1))
    inv_all = lax.rsqrt(square_total / width + EPSILON)
    inv_own = inv_all[0][:, None]
    gated_raw = after(gated_raw, square_total)

    def two_step(parts, cost=5, behind=False):
        diag = rows_terms(parts, (3,), seg, cost=cost)
        first = settled(*diag) if behind else diag[0]
        rest = rows_terms(parts, (1, 2, 0), seg, (first,))
        return [rest[4], *rest[:4], *diag]

    mix_parts = [(gated_raw, (2, h), w_gates[h], chan) for h in range(2)]
    mix_sums, _ = scatter_rows(two_step(mix_parts))
    mix_raw, resid, *normed, inv_two = token_call(
        mixed_kernel,
        [*mix_sums, tok_own, inv_own, gain_two],
        [(whole, FULL), (whole, FULL), (piece, LOW), (piece, LOW), (column, FULL)],
        seg,
        width,
    )

    normed_mlp = gather_rows(normed)
    cot_pieces = lax.optimization_barrier((*cot_pieces, normed_mlp[6]))[:2]
    w_mlp = own_other(after(w_mlp, normed_mlp[2]))
    acts = [rows_acts(normed_mlp, w) for w in w_mlp]
    gate_act, up_act, hidden = zip(*acts)
    cot_all = gather_rows(cot_pieces, (hidden[1],))

    def hidden_pieces(h):
        return [(hidden[h], r * seg, seg) for r in range(4)]

    (grad_other,) = rows_grad(cot_all, [[hidden_pieces(1)]], 7)
    (grad_down,) = rows_grad(cot_all, [[hidden_pieces(0)]], 8, swap_core(grad_other))
    w_down = gather_width(after(down, normed_mlp[2]))
    w_down = own_other(after(w_down, *hidden))
    w_down[0] = after(w_down[0], grad_down)
    grad_down = scatter_width(grad_down)
    d_acts = {}

    def back_terms(picked, cost, *first):
        downs = [after(w_down[0], *first), w_down[1]] if first else w_down
        d_acts[picked], *terms = rows_back(cot_all, gate_act, up_act, downs, w_mlp, picked, seg, cost)
        return terms

    diag = back_terms((3,), 13)
    sides = back_terms((1, 2), 0, diag[0])
    mine = back_terms((0,), 0, sides[0])
    mlp_sums, sent = scatter_rows([*mine, *sides, *diag], tuple(mine))
    def d_act_pieces(h):
        return [
            (d_acts[picked], (2 * k + h) * seg, seg)
            for picked, k in (((0,), 0), ((1, 2), 0), ((1, 2), 1), ((3,), 0))
        ]

    normed_mlp[0] = after(normed_mlp[0], *sent)
    (grad_other,) = rows_grad(normed_mlp, [[d_act_pieces(1)]], 0)
    mlp_sums[0] = after(mlp_sums[0], grad_other)

    d_resid, *d_low, gain_two_sum = token_call(
        d_mlp_kernel,
        [*mlp_sums, resid, inv_two, *cot_all[:2], gain_two, mix_raw],
        [(whole, FULL), (wider, LOW), (wider, LOW), ((1, width), FULL)],
        seg,
        width,
    )
    hidden = [after(hidden[0], *d_low), hidden[1]]
    out_terms = two_step([(hidden[h], (1, 0), w_down[h], 0) for h in range(2)], 0)
    d_resid_all = gather_rows(d_low)
    normed_mlp[0] = after(normed_mlp[0], *d_low)
    (grad_mlp,) = rows_grad(normed_mlp, [[d_act_pieces(0)]], 0, swap_core(grad_other))
    d_resid_all[6] = after(d_resid_all[6], grad_mlp, *out_terms)
    grad_mlp = scatter_width(grad_mlp)
    out_terms = list(lax.optimization_barrier((*out_terms, d_resid_all[6]))[:-1])
    out_sums, sent = scatter_rows(out_terms)
    dot_total = jnp.stack([v[:, width : width + 128] for v in d_resid_all]).astype(FULL)
    dot_total = jnp.sum(dot_total, axis=-1).reshape(4, seg)
    d_gated = rows_dot(d_resid_all, w_gates, chan, chan)
    gated, d_proj_gate, gain_three_grad, back_local, back_prod = channel_call(
        functools.partial(gate_back_kernel, seg, width),
        [
            d_gated,
            proj_gate,
            state,
            gain_three,
            columns(inv_all),
            columns(dot_total),
            after(decay, grad_down),
        ],
        [((8 * seg, chan), LOW)] * 2 + [((8, chan), FULL)] + [channel] * 2,
        [((8 * seg, 128), FULL)],
    )
    both = [
        rows_grad(xs, [[block_pieces(v, h, seg)] for h in range(2)], 0, None, width)
        for xs, v in ((normed_in, d_proj_gate), (d_resid_all, gated))
    ]
    grad_gates = [jnp.concatenate([v[h] for v in both], axis=1) for h in range(2)]
    first_decay = by_row(decay)[:, 0]
    returned = enter(
        first_decay * by_row(back_prod)[:, 0],
        first_decay * by_row(back_local)[:, 0],
        segments,
        True,
    )

    def chip_sum(own, other):
        return (own.astype(FULL) + swap_core(other).astype(FULL)).astype(LOW)

    grad_gates = chip_sum(*grad_gates)
    mlp_places = rows_by_place(jnp.concatenate([grad_mlp, grad_down], axis=1), batch)
    returned = after(returned, grad_gates, *mlp_places, *out_sums)
    grad_gates = scatter_width(grad_gates)
    *d_scan, bound_grad = channel_call(
        functools.partial(scan_back_kernel, seg),
        [
            back_local,
            back_prod,
            returned,
            state,
            carry_in,
            proj_in,
            proj_forget,
            bound,
            keep_mask,
        ],
        [((8 * seg, chan), LOW), ((8 * seg, chan), LOW), ((8, chan), FULL)],
    )
    grad_scan = rows_grad(
        normed_in, [[block_pieces(v, h, seg) for v in d_scan] for h in range(2)], 0
    )
    grad_scan = chip_sum(*grad_scan)
    d_scan[0] = after(d_scan[0], grad_scan)
    grad_scan = scatter_width(grad_scan)
    in_parts = [(d_scan[k], (2, h), w_scan[h], k * chan) for h in range(2) for k in range(2)]
    in_parts += [(d_proj_gate, (2, h), w_gates[h], 0) for h in range(2)]
    in_sums, sent = scatter_rows(two_step(in_parts, 5, True), (grad_gates,))
    in_sums[0] = after(in_sums[0], grad_scan)
    behind = settled(*sent)
    mlp = exchange(list(lax.optimization_barrier((*mlp_places, behind))[:4]))
    grad_own, gain_one_sum = token_call(
        d_in_kernel,
        [*in_sums, tok_own, inv_one, gain_one, d_resid],
        [(whole, FULL), ((1, width), FULL)],
        seg,
        width,
        0,
    )
    mixer = exchange(rows_by_place(jnp.concatenate([grad_scan, grad_gates], axis=1), batch))

    def own_rest(v):
        return (
            lax.dynamic_index_in_dim(v, core, 0, keepdims=False),
            lax.dynamic_index_in_dim(v, 1 - core, 0, keepdims=False),
        )

    (out_own,) = token_call(out_kernel, [*out_sums, after(resid, grad_own)], [(whole, LOW)], seg, width)
    out_keep, out_send = own_rest(jnp.stack([out_own[:, :half], out_own[:, half:]]))
    tokens_out = both_rows(core, out_keep, swap_core(out_send))

    gains = jnp.concatenate([gain_one_sum, gain_two_sum]).reshape(2, 2, half)
    gains_keep, gains_send = own_rest(jnp.swapaxes(gains, 0, 1))
    channels = lax.dynamic_update_slice_in_dim(
        jnp.zeros((2, 2, half), FULL),
        jnp.sum(jnp.stack([gain_three_grad, bound_grad]).reshape(2, 4, 2, chan), axis=1).swapaxes(0, 1),
        batch * chan,
        2,
    )
    small = jnp.concatenate([gains_keep, channels[0]]) + swap_core(
        jnp.concatenate([gains_send, channels[1]])
    )
    small = sum_all(after(small, *mlp), segments)
    soft = jax.nn.softmax(bound_param, axis=0)
    grad_table = small[3] * soft * (used - jnp.sum(soft * used, axis=0))
    *grads, grad_tokens = final(
        batch, core, mlp, mixer, grad_own, swap_core(grad_own), half, 4 * unit, (behind,)
    )
    return (tokens_out, grad_tokens, *grads, small[0], small[1], small[2], grad_table)


def solution(mesh):
    return jax.shard_map(
        shards,
        mesh=mesh,
        in_specs=(
            P("batch", "seq", None),
            P("batch", "seq", None),
            P(("seq", "batch"), "mp"),
            P(("seq", "batch"), "mp"),
            P(("seq", "batch"), "mp"),
            P("mp", ("seq", "batch")),
            P(("seq", "batch"), "mp"),
            P(("seq", "batch"), "mp"),
            P("mp", ("seq", "batch")),
            P(),
            P(),
            P("mp"),
            P(None, "mp"),
            P(),
            P("batch", None),
        ),
        out_specs=(
            P("batch", "seq", "mp"),
            P("batch", "seq", None),
            P(("seq", "batch"), "mp"),
            P(("seq", "batch"), "mp"),
            P(("seq", "batch"), "mp"),
            P("mp", ("seq", "batch")),
            P(("seq", "batch"), "mp"),
            P(("seq", "batch"), "mp"),
            P("mp", ("seq", "batch")),
            P("mp"),
            P("mp"),
            P("mp"),
            P(None, "mp"),
        ),
        check_vma=False,
    )
```

```python
import functools

import jax
import jax.numpy as jnp
from jax import lax
from jax.experimental import pallas as pl
from jax.experimental.pallas import tpu as pltpu
from jax.sharding import PartitionSpec as P

EPSILON = 1e-06
LOW = jnp.bfloat16
FULL = jnp.float32
VMEM_BYTES = 56 * 1024 * 1024
ANYWHERE = pl.BlockSpec(memory_space=pl.ANY)


def swap_x(v):
    return lax.ppermute(v, "batch", [(i, i ^ 1) for i in range(4)])


def swap_y(v):
    return lax.ppermute(v, "batch", [(i, i ^ 2) for i in range(4)])


def swap_xy(v):
    return lax.ppermute(v, "batch", [(i, i ^ 3) for i in range(4)])


def swap_core(v):
    return lax.ppermute(v, "mp", [(0, 1), (1, 0)])


def after(v, *first):
    return lax.optimization_barrier((v, *first))[0]


def settled(*first):
    return swap_core(lax.optimization_barrier(first)[0][:16, :128])


def contract(left, right, left_dim, right_dim):
    return lax.dot_general(
        left, right, (((left_dim,), (right_dim,)), ((), ())), preferred_element_type=FULL
    )


def by_place(blocks, batch):
    stacked = jnp.stack(blocks)
    return [
        lax.dynamic_index_in_dim(stacked, jnp.bitwise_xor(batch, a), 0, keepdims=False)
        for a in range(4)
    ]


def exchange(blocks):
    return [blocks[0], swap_x(blocks[1]), swap_y(blocks[2]), swap_xy(blocks[3])]


def hidden_blocks(weights, batch):
    places = [
        jnp.concatenate(
            [w[:, a * (w.shape[1] // 4) : (a + 1) * (w.shape[1] // 4)] for w in weights], axis=1
        )
        for a in range(4)
    ]
    return lax.optimization_barrier(exchange(by_place(places, batch)))


def gather_width(shard):
    return lax.all_gather(shard, "seq", axis=0, tiled=True)


def shard_of(blocks, batch):
    return jnp.concatenate(by_place(blocks, batch), axis=0)


def scatter_width(grad):
    return lax.psum_scatter(grad, "seq", scatter_dimension=0, tiled=True)


def rows_by_place(part, batch):
    rows = part.shape[0] // 4
    return by_place([part[a * rows : (a + 1) * rows] for a in range(4)], batch)


def gather_rows(own, then=(), between=()):
    first, last = own
    late_first, late_last = lax.optimization_barrier((first, last, *between))[:2]
    x_first, y_last, x_last, y_first = lax.optimization_barrier(
        (swap_x(first), swap_y(last), swap_x(late_last), swap_y(late_first), *then)
    )[:4]
    d_first, d_last = lax.optimization_barrier((swap_y(x_first), swap_x(y_last)))
    return [first, last, x_first, x_last, y_first, y_last, d_first, d_last]


def scatter_rows(terms, then=()):
    mine, x_first, x_last, y_first, y_last, d_first, d_last = terms
    by_x, by_y, gx_first, gy_last = lax.optimization_barrier(
        (swap_x(d_first), swap_y(d_last), swap_x(x_first), swap_y(y_last), *then)
    )[:4]
    x_last = (x_last + by_y.astype(FULL)).astype(LOW)
    y_first = (y_first + by_x.astype(FULL)).astype(LOW)
    gx_last, gy_first = lax.optimization_barrier((swap_x(x_last), swap_y(y_first)))
    return [mine, gx_first, gx_last, gy_first, gy_last], (x_last, y_first)


def sum_tokens(v):
    got = swap_x(v)
    v = v + jnp.stack([got[1], got[0], got[3], got[2]])
    got = swap_y(v)
    return v + jnp.stack([got[2], got[3], got[0], got[1]])


def sum_all(v, count):
    v = (v + swap_x(v)) + (swap_y(v) + swap_xy(v))
    step = 1
    while step < count:
        got = [
            lax.ppermute(v, "seq", [(i, i ^ (k * step)) for i in range(count)])
            for k in (1, 2, 3)
            if k * step < count
        ]
        v = v + got[0] if len(got) < 3 else (v + got[0]) + (got[1] + got[2])
        step *= 4
    return v


def enter(product, last, count, back, hops):
    def shift(pair, k):
        hops = [(i, i + k) for i in range(count - k)]
        return lax.ppermute(pair, "seq", [(b, a) for a, b in hops] if back else hops)

    def link(earlier, later):
        return jnp.stack([earlier[0] * later[0], later[0] * earlier[1] + later[1]])

    ends = jnp.stack([product, last])
    value = shift(ends, 1)
    hops.append(value)
    step = 2
    while step < count:
        value = link(shift(link(value, ends), step), value)
        step *= 2
    return value[1]


def call(kernel, arrays, outs, scratch, cost, first=()):
    count = len(arrays)
    arrays = [*arrays, *first]

    def body(*refs):
        kernel(*refs[:count], *refs[len(arrays) :])

    return pl.pallas_call(
        body,
        in_specs=[ANYWHERE] * len(arrays),
        out_specs=[ANYWHERE] * len(outs),
        out_shape=[jax.ShapeDtypeStruct(shape, kind) for shape, kind in outs],
        scratch_shapes=[
            pltpu.SemaphoreType.DMA(v) if isinstance(v[0], int) else pltpu.VMEM(*v) for v in scratch
        ],
        compiler_params=pltpu.CompilerParams(vmem_limit_bytes=VMEM_BYTES),
        cost_estimate=pl.CostEstimate(
            flops=int(cost * 1.1e9), bytes_accessed=0, transcendentals=0
        ),
    )(*arrays)


def copy_in(source, target, sem):
    copy = pltpu.make_async_copy(source, target, sem)
    copy.start()
    return copy


def wait_all(copies):
    for copy in copies:
        copy.wait()


def dot_kernel(n, first, wide, *refs):
    xs, ws, out, (x_s, w_s, o_s, x_sem, w_sem, out_sem) = (
        refs[: 2 * n],
        refs[2 * n : 2 * n + 2],
        refs[2 * n + 2],
        refs[2 * n + 3 :],
    )
    rows = x_s.shape[1] // 2
    cols = pl.ds(first, wide)
    loads_w = [copy_in(ws[0].at[:, cols], w_s.at[0], w_sem.at[0])]
    loads = []
    for p, x in enumerate(xs):
        x = x.at[:, pl.ds(0, x_s.shape[2])]
        loads.append(copy_in(x, x_s.at[p // 2, pl.ds(p % 2 * rows, rows)], x_sem.at[p]))
        if p == 1:
            loads_w.append(copy_in(ws[1].at[:, cols], w_s.at[1], w_sem.at[1]))
    stores = []
    for r in range(n):
        wait_all(loads[2 * r : 2 * r + 2])
        for h in range(2):
            if r == 0:
                loads_w[h].wait()
            o_s[2 * r + h] = contract(x_s[r], w_s[h], 1, 0)
            at = pl.ds((2 * r + h) * 2 * rows, 2 * rows)
            stores.append(copy_in(o_s.at[2 * r + h], out.at[at], out_sem.at[2 * r + h]))
    wait_all(stores)


def rows_dot(xs, ws, first, wide, cost=0, behind=()):
    n, rows, depth = len(xs) // 2, xs[0].shape[0], ws[0].shape[0]
    return call(
        functools.partial(dot_kernel, n, first, wide),
        [*xs, *ws],
        [((4 * n * rows, wide), FULL)],
        [
            ((n, 2 * rows, depth), LOW),
            ((2, depth, wide), LOW),
            ((2 * n, 2 * rows, wide), FULL),
            (2 * n,),
            (2,),
            (2 * n,),
        ],
        cost,
        behind,
    )[0]


def acts_kernel(n, *refs):
    xs, w, outs, held, (x_s, w_s, sem, out_sem) = (
        refs[: 2 * n],
        refs[2 * n],
        refs[2 * n + 1 : 2 * n + 4],
        refs[2 * n + 4 : 2 * n + 7],
        refs[2 * n + 7 :],
    )
    rows, unit = x_s.shape[1] // 2, held[0].shape[1]
    load_w = copy_in(w, w_s, sem.at[2 * n])
    loads = [
        copy_in(x, x_s.at[p // 2, pl.ds(p % 2 * rows, rows)], sem.at[p]) for p, x in enumerate(xs)
    ]
    load_w.wait()
    stores = []
    for r in range(n):
        wait_all(loads[2 * r : 2 * r + 2])
        acts = contract(x_s[r], w_s[...], 1, 0)
        g, u = acts[:, :unit], acts[:, unit:]
        at = pl.ds(r * 2 * rows, 2 * rows)
        held[0][at, :] = g
        held[1][at, :] = u
        held[2][at, :unit] = (g * jax.nn.sigmoid(g) * u).astype(LOW)
        held[2][at, unit:] = jnp.zeros((2 * rows, held[2].shape[1] - unit), LOW)
        for k in range(3):
            stores.append(copy_in(held[k].at[at], outs[k].at[at], out_sem.at[r, k]))
    wait_all(stores)


def rows_acts(xs, w):
    n, (rows, depth), unit = len(xs) // 2, xs[0].shape, w.shape[1] // 2
    padded = pl.cdiv(unit, 128) * 128
    outs = [((2 * n * rows, v), kind) for v, kind in ((unit, FULL), (unit, FULL), (padded, LOW))]
    return call(
        functools.partial(acts_kernel, n),
        [*xs, w],
        outs,
        [*outs, ((n, 2 * rows, depth), LOW), (w.shape, LOW), (2 * n + 1,), (n, 3)],
        0,
    )


def grad_kernel(x_at, y_at, more, *refs):
    n = len(y_at)
    outs, (x_s, y_s, m_s), held = refs[-5 - 2 * n - 2 : -5 - n - 2], refs[-5 - n - 2 : -4 - n], refs[-4 - n : -4]
    x_sem, y_sem, m_sem, out_sem = refs[-4:]
    wide = held[0].shape[1]
    chunks = [chunk for group in y_at for chunk in group]
    each = y_s.shape[1] // len(chunks)
    loads = []
    for g, (target, places) in enumerate(((x_s, x_at), *[(y_s, v) for v in chunks])):
        start = 0
        for k, (i, first, rows) in enumerate(places):
            at = target.at[pl.ds(start, rows)]
            if g:
                at = target.at[pl.ds(start, rows), pl.ds((g - 1) * each, each)]
            sem = y_sem.at[g - 1, k] if g else x_sem.at[k]
            source = refs[i].at[pl.ds(first, rows), pl.ds(0, at.shape[1])]
            loads.append(copy_in(source, at, sem))
            start += rows
    if more is not None:
        load_more = copy_in(refs[more], m_s, m_sem.at[0])
    wait_all(loads)
    depth, stores = x_s.shape[1], []
    for block, first in enumerate(range(0, depth, 256)):
        cols = pl.ds(first, min(256, depth - first))
        total = contract(x_s[:, cols], y_s[...], 0, 0)
        if more is not None:
            if block == 0:
                load_more.wait()
            total = total + m_s[cols, :].astype(FULL)
        for g in range(n):
            held[g][cols, :] = total[:, g * wide : (g + 1) * wide].astype(LOW)
            stores.append(copy_in(held[g].at[cols], outs[g].at[cols], out_sem.at[g, block]))
    wait_all(stores)


def rows_grad(xs, groups, cost, more=None, depth=None):
    arrays, x_at, y_at = list(xs), [(k, 0, x.shape[0]) for k, x in enumerate(xs)], []
    for group in groups:
        y_at.append([])
        for chunk in group:
            y_at[-1].append([])
            for v, first, rows in chunk:
                found = [k for k, other in enumerate(arrays) if other is v]
                if not found:
                    found = [len(arrays)]
                    arrays.append(v)
                y_at[-1][-1].append((found[0], first, rows))
    count = sum(rows for _, _, rows in x_at)
    depth = depth or xs[0].shape[1]
    n, each = len(groups), groups[0][0][0][0].shape[1]
    wide = each * len(groups[0])
    at = None
    if more is not None:
        at = len(arrays)
        arrays.append(more)
    outs = [((depth, wide), LOW)] * n
    return call(
        functools.partial(grad_kernel, x_at, y_at, at),
        arrays,
        outs,
        [
            ((count, depth), LOW),
            ((count, n * wide), LOW),
            ((depth if more is not None else 16, wide), LOW),
            *outs,
            (len(x_at),),
            (n * len(groups[0]), len(y_at[0][0])),
            (1,),
            (n, pl.cdiv(depth, 256)),
        ],
        cost,
    )


def block_pieces(v, half, seg):
    return [(v, (2 * r + half) * seg, seg) for r in range(4)]


PIECES = (((0, 2, FULL),), ((0, 1, LOW), (1, 2, FULL)), ((0, 1, FULL), (1, 2, LOW)), ((0, 1, LOW), (1, 2, LOW)))


def term_outs(picked, seg, wide):
    return [
        (((b - a) * seg // 2, wide), kind) for r in picked for a, b, kind in PIECES[r]
    ]


def store_term(term, r, seg, held, outs, sem, start):
    stores = []
    for k, (a, b, kind) in enumerate(PIECES[r]):
        held[start + k][...] = term[a * seg // 2 : b * seg // 2].astype(kind)
        stores.append(copy_in(held[start + k], outs[start + k], sem.at[start + k]))
    return stores


def term_kernel(picked, parts, count, *refs):
    n = sum(len(PIECES[r]) for r in picked)
    arrays, outs, held = refs[:count], refs[count : count + n], refs[count + n : count + 2 * n]
    scratch = refs[count + 2 * n :]
    l_s, w_s = scratch[: len(parts)], scratch[len(parts) : 2 * len(parts)]
    l_sem, w_sem, out_sem = scratch[2 * len(parts) :]
    seg = l_s[0].shape[1]
    loads, loads_w = [], []
    for k, r in enumerate(picked):
        loads.append([])
        for p, (left, (each, half), w, first, depth) in enumerate(parts):
            if k == 0:
                source = arrays[w].at[:, pl.ds(first, depth)]
                loads_w.append(copy_in(source, w_s[p], w_sem.at[p]))
            at = pl.ds((each * r + half) * seg, seg)
            loads[k].append(copy_in(arrays[left].at[at], l_s[p].at[k], l_sem.at[k, p]))
    stores, start = [], 0
    for k, r in enumerate(picked):
        term = None
        for p in range(len(parts)):
            loads[k][p].wait()
            if k == 0:
                loads_w[p].wait()
            part = contract(l_s[p][k], w_s[p][...], 1, 1)
            term = part if term is None else term + part
        stores += store_term(term, r, seg, held, outs, out_sem, start)
        start += len(PIECES[r])
    wait_all(stores)


def rows_terms(parts, picked, seg, first=(), cost=0):
    arrays, places = [], []
    for left, block, w, column in parts:
        at = []
        for v in (left, w):
            found = [k for k, other in enumerate(arrays) if other is v]
            if not found:
                found = [len(arrays)]
                arrays.append(v)
            at.append(found[0])
        places.append((at[0], block, at[1], column, left.shape[1]))
    wide = parts[0][2].shape[0]
    outs = term_outs(picked, seg, wide)
    return call(
        functools.partial(term_kernel, picked, places, len(arrays)),
        arrays,
        outs,
        [
            *outs,
            *[((len(picked), seg, depth), LOW) for *_, depth in places],
            *[((wide, depth), LOW) for *_, depth in places],
            (len(picked), len(parts)),
            (len(parts),),
            (len(outs),),
        ],
        cost,
        first,
    )


def back_kernel(picked, *refs):
    n = len(picked)
    m = sum(len(PIECES[r]) for r in picked)
    dys, gates, ups, downs, mlps, d_acts = (
        refs[: 2 * n],
        refs[2 * n : 2 * n + 2],
        refs[2 * n + 2 : 2 * n + 4],
        refs[2 * n + 4 : 2 * n + 6],
        refs[2 * n + 6 : 2 * n + 8],
        refs[2 * n + 8],
    )
    outs, held = refs[2 * n + 9 : 2 * n + 9 + m], refs[2 * n + 9 + m : 2 * n + 9 + 2 * m]
    y_s, g_s, u_s, down_s, mlp_s, a_s, y_sem, act_sem, w_sem, a_sem, out_sem = refs[
        2 * n + 9 + 2 * m :
    ]
    seg, unit = g_s.shape[2:]
    loads_w, loads_y, loads_act = [], [], []
    for k, r in enumerate(picked):
        at = pl.ds(r * seg, seg)
        loads_y.append(
            [
                copy_in(
                    dys[2 * k + p], y_s.at[k, pl.ds(p * seg // 2, seg // 2)], y_sem.at[k, p]
                )
                for p in range(2)
            ]
        )
        loads_act.append([])
        for h in range(2):
            if k == 0:
                loads_w.append(copy_in(downs[h], down_s.at[h], w_sem.at[h, 0]))
            loads_act[k].append(
                [
                    copy_in(gates[h].at[at], g_s.at[k, h], act_sem.at[k, h, 0]),
                    copy_in(ups[h].at[at], u_s.at[k, h], act_sem.at[k, h, 1]),
                ]
            )
            if k == 0:
                loads_w.append(copy_in(mlps[h], mlp_s.at[h], w_sem.at[h, 1]))
    stores, start = [], 0
    for k, r in enumerate(picked):
        wait_all(loads_y[k])
        term = None
        for h in range(2):
            if k == 0:
                loads_w[2 * h].wait()
            d_hidden = contract(y_s[k], down_s[h], 1, 0)[:, :unit]
            wait_all(loads_act[k][h])
            g, u = g_s[k, h], u_s[k, h]
            sig = jax.nn.sigmoid(g)
            a_s[k, h, :, :unit] = (d_hidden * u * sig * (1.0 + g * (1.0 - sig))).astype(LOW)
            a_s[k, h, :, unit:] = (d_hidden * (g * sig)).astype(LOW)
            at = pl.ds((2 * k + h) * seg, seg)
            stores.append(copy_in(a_s.at[k, h], d_acts.at[at], a_sem.at[k, h]))
            if k == 0:
                loads_w[2 * h + 1].wait()
            part = contract(a_s[k, h], mlp_s[h], 1, 1)
            term = part if term is None else term + part
        stores += store_term(term, r, seg, held, outs, out_sem, start)
        start += len(PIECES[r])
    wait_all(stores)


def rows_back(dys, gates, ups, downs, mlps, picked, seg, cost):
    n, (wide, both) = len(picked), mlps[0].shape
    unit = both // 2
    outs = term_outs(picked, seg, wide)
    return call(
        functools.partial(back_kernel, picked),
        [*[dys[2 * r + p] for r in picked for p in range(2)], *gates, *ups, *downs, *mlps],
        [((2 * n * seg, both), LOW), *outs],
        [
            *outs,
            ((n, seg, wide), LOW),
            ((n, 2, seg, unit), FULL),
            ((n, 2, seg, unit), FULL),
            ((2, *downs[0].shape), LOW),
            ((2, wide, both), LOW),
            ((n, 2, seg, both), LOW),
            (n, 2),
            (n, 2, 2),
            (2, 2),
            (n, 2),
            (len(outs),),
        ],
        cost,
    )


def channel_call(kernel, arrays, outs, scratch=(), cost=0):
    def spec(shape, skip=0):
        if shape[1] == 1:
            return pl.BlockSpec(shape, lambda i: (0, 0))
        if skip == shape[1] // 128 - 1:
            return pl.BlockSpec((shape[0], 128), lambda i: (0, skip))
        return pl.BlockSpec((shape[0], 128), lambda i: (0, i + skip))

    skips = [v[1] if isinstance(v, tuple) else 0 for v in arrays]
    arrays = [v[0] if isinstance(v, tuple) else v for v in arrays]

    return pl.pallas_call(
        kernel,
        grid=(2,),
        in_specs=[spec(v.shape, skip) for v, skip in zip(arrays, skips)],
        out_specs=[spec(shape) for shape, _ in outs],
        out_shape=[jax.ShapeDtypeStruct(shape, kind) for shape, kind in outs],
        scratch_shapes=[pltpu.VMEM(*v) for v in scratch],
        compiler_params=pltpu.CompilerParams(vmem_limit_bytes=VMEM_BYTES),
        cost_estimate=pl.CostEstimate(
            flops=int(cost * 1.1e9), bytes_accessed=0, transcendentals=0
        ),
    )(*arrays)


def forward_scan(seg, rows, decay_ref, input_ref, state_ref, product_ref):
    def body(t, carry):
        h, p = carry
        at = pl.ds(t, rows, stride=seg)
        d = decay_ref[at, :]
        h = d * h + input_ref[at, :]
        p = d * p
        state_ref[at, :] = h
        product_ref[at, :] = p
        return h, p

    first = pl.ds(0, rows, stride=seg)
    h, p = input_ref[first, :], decay_ref[first, :]
    state_ref[first, :] = h
    product_ref[first, :] = p
    lax.fori_loop(1, seg, body, (h, p), unroll=5)


def backward_scan(seg, rows, decay_ref, input_ref, state_ref, product_ref):
    def body(k, carry):
        h, p, d = carry
        at = pl.ds(seg - 1 - k, rows, stride=seg)
        h = d * h + input_ref[at, :]
        p = d * p
        state_ref[at, :] = h
        product_ref[at, :] = p
        return h, p, decay_ref[at, :]

    last = pl.ds(seg - 1, rows, stride=seg)
    h, p = input_ref[last, :], decay_ref[last, :]
    state_ref[last, :] = h
    product_ref[last, :] = jnp.ones_like(p)
    at = pl.ds(seg - 2, rows, stride=seg)
    h = p * h + input_ref[at, :]
    state_ref[at, :] = h
    product_ref[at, :] = p
    lax.fori_loop(2, seg, body, (h, p, decay_ref[at, :]), unroll=2)


def scan_kernel(seg, proj_in, proj_forget, bound, keep, decay, local, product, inputs):
    rows = bound.shape[0]
    for k in range(rows):
        at = pl.ds(k * seg, seg)
        low = bound[pl.ds(k, 1), :]
        forget = low + (1.0 - low) * jax.nn.sigmoid(proj_forget[at, :])
        v = proj_in[at, :]
        decay[at, :] = forget * keep[at, :]
        inputs[at, :] = v * jax.nn.sigmoid(v) * (1.0 - forget)
    forward_scan(seg, rows, decay, inputs, local, product)


def state_kernel(seg, local, product, carry, gate, gain, state, gated, squares):
    first = pl.program_id(0) == 0
    for k in range(carry.shape[0]):
        at, one = pl.ds(k * seg, seg), pl.ds(k, 1)
        h = local[at, :] + product[at, :] * carry[one, :]
        g = gate[at, :]
        state[at, :] = h
        gated[at, :] = (h * gain[one, :] * (g * jax.nn.sigmoid(g))).astype(LOW)
        total = jnp.sum(h * h, axis=-1, keepdims=True)
        squares[at, :] = jnp.where(first, 0.0, squares[at, :]) + total


def gate_back_kernel(
    seg, wide, d_gated, gate, state, gain, inverse, *refs
):
    dots, (decay, gated, d_gate, gain_sum, local, product, held) = refs[:8], refs[8:]
    rows = gain.shape[0]
    for k in range(rows):
        at, one = pl.ds(k * seg, seg), pl.ds(k, 1)
        up, g, h, scale, inv = d_gated[at, :], gate[at, :], state[at, :], gain[one, :], inverse[at, :]
        sig = jax.nn.sigmoid(g)
        act, normed = g * sig, h * inv
        gated[at, :] = (normed * scale * act).astype(LOW)
        d_gate[at, :] = (up * normed * scale * sig * (1.0 + g * (1.0 - sig))).astype(LOW)
        gain_sum[one, :] = jnp.sum(up * normed * act, axis=0, keepdims=True)
        dot = jnp.concatenate([dots[k // 2 * 2 + p][...].astype(FULL) for p in range(2)])
        dot = jnp.sum(dot, axis=1, keepdims=True)
        shrink = inv * inv * inv * (dot * (1.0 / wide))
        held[at, :] = inv * (up * scale * act) - h * shrink
    backward_scan(seg, rows, decay, held, local, product)


def scan_back_kernel(
    seg, local, product, returned, state, carry, proj_in, proj_forget, bound, keep, d_in_ref, d_forget_ref, bound_sum
):
    for k in range(bound.shape[0]):
        at, one = pl.ds(k * seg, seg), pl.ds(k, 1)
        lam = local[at, :] + product[at, :] * returned[one, :]
        h = state[at, :]
        step = lax.broadcasted_iota(jnp.int32, h.shape, 0)
        previous = jnp.where(step == 0, carry[one, :], pltpu.roll(h, 1, 0))
        low, v = bound[one, :], proj_in[at, :]
        sig_forget, sig_in = jax.nn.sigmoid(proj_forget[at, :]), jax.nn.sigmoid(v)
        forget = low + (1.0 - low) * sig_forget
        d_forget = lam * (previous * keep[at, :] - v * sig_in)
        d_in = lam * (1.0 - forget) * sig_in * (1.0 + v * (1.0 - sig_in))
        d_in_ref[at, :] = d_in.astype(LOW)
        d_forget_ref[at, :] = (d_forget * (1.0 - low) * sig_forget * (1.0 - sig_forget)).astype(LOW)
        bound_sum[one, :] = jnp.sum(d_forget * (1.0 - sig_forget), axis=0, keepdims=True)


STEP = 32


def token_call(kernel, arrays, outs, seg, wide, cost=0):
    half = seg // 2

    def spec(shape):
        if shape[0] == 1:
            return pl.BlockSpec(shape, lambda i: (0, 0))
        if shape[0] == 2:
            return pl.BlockSpec((2, STEP, shape[2]), lambda i: (0, i, 0))
        return pl.BlockSpec((STEP, shape[1]), lambda i: (i, 0))

    def folded(shape):
        return (2, half, shape[1]) if shape[0] == seg else shape

    arrays = [v.reshape(folded(v.shape)) for v in arrays]
    got = pl.pallas_call(
        kernel,
        grid=(half // STEP,),
        in_specs=[spec(v.shape) for v in arrays],
        out_specs=[spec(folded(shape)) for shape, _ in outs],
        out_shape=[jax.ShapeDtypeStruct(folded(shape), kind) for shape, kind in outs],
        compiler_params=pltpu.CompilerParams(vmem_limit_bytes=VMEM_BYTES),
        cost_estimate=pl.CostEstimate(
            flops=int(cost * 1.1e9), bytes_accessed=0, transcendentals=0
        ),
    )(*arrays)
    return [v.reshape(shape) for v, (shape, _) in zip(got, outs)]


def both_rows(core, mine, got):
    return jnp.where(core == 0, jnp.stack([mine, got]), jnp.stack([got, mine]))


def final_kernel(place, core, *refs):
    mlp, mixer, (mine, got), refs = refs[:4], refs[4:8], refs[8:10], refs[10:]
    outs, (m_s, x_s, t_s), refs = refs[:8], refs[8:11], refs[11:]
    held, (sem, out_sem) = refs[:7], refs[7:]
    rows = [copy_in(v, t_s.at[k], sem.at[8 + k]) for k, v in enumerate((mine, got))]
    loads = [copy_in(v, m_s.at[k], sem.at[k]) for k, v in enumerate(mlp)]
    loads += [copy_in(v, x_s.at[k], sem.at[4 + k]) for k, v in enumerate(mixer)]
    wait_all(rows)
    stores = [
        copy_in(t_s.at[0], outs[7].at[core[0]], out_sem.at[7]),
        copy_in(t_s.at[1], outs[7].at[1 - core[0]], out_sem.at[8]),
    ]
    wait_all(loads)
    chan, unit = held[0].shape[1] // 4, held[4].shape[1] // 4
    for a in range(4):
        block = jnp.bitwise_xor(place[0], a)
        m, x = m_s[block].astype(FULL), x_s[block].astype(FULL)
        for k in range(3):
            held[k][:, a * chan : (a + 1) * chan] = x[:, k * chan : (k + 1) * chan]
        held[3][a * chan : (a + 1) * chan, :] = x[:, 3 * chan : 4 * chan].T
        for k in range(2):
            held[4 + k][:, a * unit : (a + 1) * unit] = m[:, k * unit : (k + 1) * unit]
        held[6][a * unit : (a + 1) * unit, :] = m[:, 2 * unit : 3 * unit].T
    stores += [copy_in(held[k], outs[k], out_sem.at[k]) for k in range(7)]
    wait_all(stores)


def final(place, core, mlp, mixer, mine, got, half, hidden, first):
    rows = mixer[0].shape[0]
    outs = [((rows, half), FULL)] * 3 + [((half, rows), FULL)]
    outs += [((rows, hidden), FULL)] * 2 + [((hidden, rows), FULL)]
    arrays = [*mlp, *mixer, mine, got, *first]
    more = [((2, *mine.shape), FULL)]

    def body(place_ref, core_ref, *refs):
        final_kernel(place_ref, core_ref, *refs[:10], *refs[len(arrays) :])

    return pl.pallas_call(
        body,
        in_specs=[pl.BlockSpec(memory_space=pltpu.SMEM)] * 2 + [ANYWHERE] * len(arrays),
        out_specs=[ANYWHERE] * 8,
        out_shape=[jax.ShapeDtypeStruct(shape, kind) for shape, kind in outs + more],
        scratch_shapes=[
            pltpu.VMEM((4, *mlp[0].shape), LOW),
            pltpu.VMEM((4, *mixer[0].shape), LOW),
            pltpu.VMEM((2, *mine.shape), FULL),
            *[pltpu.VMEM(*v) for v in outs],
            pltpu.SemaphoreType.DMA((10,)),
            pltpu.SemaphoreType.DMA((9,)),
        ],
        compiler_params=pltpu.CompilerParams(vmem_limit_bytes=VMEM_BYTES),
    )(place.reshape(1), core.reshape(1), *arrays)


def total_of(refs, h):
    mine, gx_first, gx_last, gy_first, gy_last = refs
    got_x, got_y = ((gx_first, gy_first), (gx_last, gy_last))[h]
    return mine[h] + got_x[...].astype(FULL) + got_y[...].astype(FULL)


def inverse_of(v):
    return lax.rsqrt(jnp.mean(v * v, axis=-1, keepdims=True) + EPSILON)


def enter_kernel(tok, gain, first, last, inverse):
    for h, out in enumerate((first, last)):
        v = tok[h].astype(FULL)
        inv = inverse_of(v)
        out[...] = (v * inv * gain[...]).astype(LOW)
        inverse[h] = inv


def mixed_kernel(*refs):
    *sums, tok, inv_state, gain, mix, resid, first, last, inverse = refs
    for h, out in enumerate((first, last)):
        raw = total_of(sums, h)
        v = tok[h].astype(FULL) + inv_state[h] * raw
        inv = inverse_of(v)
        mix[h] = raw
        resid[h] = v
        out[...] = (v * inv * gain[...]).astype(LOW)
        inverse[h] = inv


def norm_back(upstream, v, scale, inv):
    weighted = upstream * scale
    mean = jnp.mean(weighted * v, axis=-1, keepdims=True)
    return inv * weighted - v * (inv * inv * inv * mean)


def add_rows(ref, v):
    total = jnp.sum(v, axis=0, keepdims=True)

    @pl.when(pl.program_id(0) == 0)
    def _():
        ref[...] = jnp.zeros_like(ref)

    ref[...] += total


def d_mlp_kernel(*refs):
    *sums, resid, inverse, cot_first, cot_last, gain, mix, d_resid, first, last, gain_sum = refs
    terms = 0.0
    for h, (cot, out) in enumerate(((cot_first, first), (cot_last, last))):
        up, v, inv = total_of(sums, h), resid[h], inverse[h]
        terms = terms + up * v * inv
        grad = cot[...].astype(FULL) + norm_back(up, v, gain[...], inv)
        low = grad.astype(LOW)
        d_resid[h] = grad
        wide = low.shape[1]
        out[:, :wide] = low
        dot = jnp.sum(low.astype(FULL) * mix[h], axis=-1, keepdims=True)
        high = dot.astype(LOW)
        dot = dot - high.astype(FULL)
        middle = dot.astype(LOW)
        rest = (dot - middle.astype(FULL)).astype(LOW)
        lane = lax.broadcasted_iota(jnp.int32, (low.shape[0], 128), 1)
        parts = jnp.where(lane == 1, middle.astype(FULL), jnp.where(lane == 2, rest.astype(FULL), 0.0))
        out[:, wide:] = jnp.where(lane == 0, high.astype(FULL), parts).astype(LOW)
    add_rows(gain_sum, terms)


def d_in_kernel(*refs):
    *sums, tok, inverse, gain, d_resid, grad, gain_sum = refs
    terms = 0.0
    for h in range(2):
        up, v, inv = total_of(sums, h), tok[h].astype(FULL), inverse[h]
        terms = terms + up * v * inv
        grad[h] = d_resid[h] + norm_back(up, v, gain[...], inv)
    add_rows(gain_sum, terms)


def out_kernel(*refs):
    *sums, resid, out = refs
    for h in range(2):
        out[h] = (resid[h] + total_of(sums, h)).astype(LOW)


def shards(
    tokens_in,
    grad_out,
    w_input,
    w_forget,
    w_outgate,
    w_out,
    mlp_gate,
    mlp_up,
    mlp_down,
    gain_mixer,
    gain_mlp,
    gain_state,
    bound_param,
    layer_index,
    doc_lengths,
):
    rows, seg, width = tokens_in.shape
    half = gain_state.shape[0]
    chan = half // 4
    unit = mlp_gate.shape[1] // 4
    segments = lax.axis_size("seq")
    core = lax.axis_index("mp")
    batch = lax.axis_index("batch")
    place = lax.axis_index("seq")
    piece = (seg // 2, width)
    wider = (seg // 2, width + 128)
    whole = (seg, width)
    column = (seg, 1)

    def own_other(v):
        return [v, swap_core(v)]

    mixer = hidden_blocks((w_input, w_forget, w_outgate, w_out.T), batch)
    shard = shard_of(mixer, batch)
    w_scan, w_gates = gather_width(shard[:, : 2 * chan]), gather_width(shard[:, 2 * chan :])
    layers = bound_param.shape[0]
    layer = jnp.arange(layers, dtype=jnp.int32)[:, None]
    used = jnp.logical_and(layer >= 1, layer <= layer_index[0]).astype(FULL)
    table = jnp.concatenate([bound_param, gain_state.astype(FULL)[None]])
    table = jnp.stack(own_other(lax.dynamic_slice_in_dim(table, batch * chan, chan, 1)))
    bound = jnp.tile(jnp.sum(jax.nn.softmax(table[:, :layers], axis=1) * used, axis=1), (4, 1))
    gain_three = jnp.tile(table[:, layers], (4, 1))
    lengths = lax.dynamic_slice_in_dim(doc_lengths, core, 1, 0)
    lengths = jnp.concatenate([lengths, swap_x(lengths)])
    lengths = jnp.concatenate([lengths, swap_y(lengths)])
    starts = jnp.cumsum(lengths, axis=1) - lengths
    places = place * seg + jnp.arange(seg, dtype=jnp.int32)
    resets = jnp.any(places[None, :, None] == starts[:, None, :], axis=2).astype(FULL)
    keep_mask = jnp.repeat(1.0 - resets, 2, axis=0).reshape(8 * seg, 1)
    mlp_blocks = hidden_blocks((after(mlp_gate, lengths, table, *mixer), mlp_up, mlp_down.T), batch)
    shard = shard_of(mlp_blocks, batch)
    w_mlp, down = gather_width(shard[:, : 2 * unit]), shard[:, 2 * unit :]
    down = jnp.pad(down, ((0, 0), (0, -unit % 128)))

    gain_one = gain_mixer.astype(FULL)[None]
    gain_two = gain_mlp.astype(FULL)[None]
    tok_own, cot_own = lax.optimization_barrier(
        [lax.dynamic_index_in_dim(v, core, 0, keepdims=False) for v in (tokens_in, grad_out)]
    )

    def by_row(v):
        return v.reshape(8, seg, chan)

    def columns(v):
        return jnp.repeat(v, 2, axis=0).reshape(8 * seg, 1)

    channel = ((8 * seg, chan), FULL)

    *normed, inv_one = token_call(
        enter_kernel,
        [tok_own, gain_one],
        [(piece, LOW), (piece, LOW), (column, FULL)],
        seg,
        width,
    )
    normed = lax.optimization_barrier((*normed, *mixer))[:2]
    normed_in = gather_rows(normed, (), mlp_blocks)
    w_scan = own_other(after(w_scan, normed_in[6]))
    proj_scan = rows_dot(normed_in, w_scan, 0, 2 * chan, 0)
    proj_in, proj_forget = (proj_scan, 0), (proj_scan, chan // 128)
    decay, local_state, cum_decay = channel_call(
        functools.partial(scan_kernel, seg),
        [proj_in, proj_forget, bound, keep_mask],
        [channel] * 3,
        [((8 * seg, 128), FULL)],
    )
    w_gates = own_other(after(w_gates, local_state))
    hops = []
    carry_in = enter(by_row(cum_decay)[:, -1], by_row(local_state)[:, -1], segments, False, hops)
    cot_pieces = [cot_own[: seg // 2], cot_own[seg // 2 :]]
    proj_gate = rows_dot(normed_in, w_gates, 0, chan, 0, (hops[0].reshape(-1, chan),))
    carry_in = after(carry_in, proj_gate)
    state, gated_raw, squares = channel_call(
        functools.partial(state_kernel, seg),
        [local_state, cum_decay, carry_in, proj_gate, gain_three],
        [channel, ((8 * seg, chan), LOW), ((8 * seg, 1), FULL)],
    )
    square_total = sum_tokens(jnp.sum(squares.reshape(4, 2, seg), axis=1))
    inv_all = lax.rsqrt(square_total / width + EPSILON)
    inv_own = inv_all[0][:, None]
    gated_raw = after(gated_raw, square_total)

    def two_step(parts, cost=0, behind=False):
        diag = rows_terms(parts, (3,), seg, cost=cost)
        first = settled(*diag) if behind else diag[0]
        rest = rows_terms(parts, (1, 2, 0), seg, (first,))
        return [rest[4], *rest[:4], *diag]

    mix_parts = [(gated_raw, (2, h), w_gates[h], chan) for h in range(2)]
    mix_sums, _ = scatter_rows(two_step(mix_parts))
    mix_raw, resid, *normed, inv_two = token_call(
        mixed_kernel,
        [*mix_sums, tok_own, inv_own, gain_two],
        [(whole, FULL), (whole, FULL), (piece, LOW), (piece, LOW), (column, FULL)],
        seg,
        width,
    )

    normed_mlp = gather_rows(normed)
    cot_pieces = lax.optimization_barrier((*cot_pieces, normed_mlp[6]))[:2]
    w_mlp = own_other(after(w_mlp, normed_mlp[2]))
    acts = [rows_acts(normed_mlp, w) for w in w_mlp]
    gate_act, up_act, hidden = zip(*acts)
    cot_all = gather_rows(cot_pieces, (hidden[1],))

    def hidden_pieces(h):
        return [(hidden[h], r * seg, seg) for r in range(4)]

    (grad_other,) = rows_grad(cot_all, [[hidden_pieces(1)]], 0)
    (grad_down,) = rows_grad(cot_all, [[hidden_pieces(0)]], 0, swap_core(grad_other))
    w_down = gather_width(after(down, normed_mlp[2]))
    w_down = own_other(after(w_down, *hidden))
    w_down[0] = after(w_down[0], grad_down)
    grad_down = scatter_width(grad_down)
    d_acts = {}

    def back_terms(picked, cost, *first):
        downs = [after(w_down[0], *first), w_down[1]] if first else w_down
        d_acts[picked], *terms = rows_back(cot_all, gate_act, up_act, downs, w_mlp, picked, seg, cost)
        return terms

    diag = back_terms((3,), 0)
    sides = back_terms((1, 2), 0, diag[0])
    mine = back_terms((0,), 0, sides[0])
    mlp_sums, sent = scatter_rows([*mine, *sides, *diag], tuple(mine))
    def d_act_pieces(h):
        return [
            (d_acts[picked], (2 * k + h) * seg, seg)
            for picked, k in (((0,), 0), ((1, 2), 0), ((1, 2), 1), ((3,), 0))
        ]

    normed_mlp[0] = after(normed_mlp[0], *sent)
    (grad_other,) = rows_grad(normed_mlp, [[d_act_pieces(1)]], 0)
    (grad_mlp,) = rows_grad(normed_mlp, [[d_act_pieces(0)]], 0, swap_core(grad_other))
    mlp_sums[0] = after(mlp_sums[0], grad_mlp)

    d_resid, *d_low, gain_two_sum = token_call(
        d_mlp_kernel,
        [*mlp_sums, resid, inv_two, *cot_all[:2], gain_two, mix_raw],
        [(whole, FULL), (wider, LOW), (wider, LOW), ((1, width), FULL)],
        seg,
        width,
        14,
    )
    hidden = [after(hidden[0], *d_low), hidden[1]]
    out_terms = two_step([(hidden[h], (1, 0), w_down[h], 0) for h in range(2)], 0)
    d_resid_all = gather_rows(d_low)
    d_resid_all[6] = after(d_resid_all[6], grad_mlp, *out_terms)
    grad_mlp = scatter_width(grad_mlp)
    out_terms = list(lax.optimization_barrier((*out_terms, d_resid_all[6]))[:-1])
    out_sums, sent = scatter_rows(out_terms)
    d_gated = rows_dot(d_resid_all, w_gates, chan, chan, 21)
    gated, d_proj_gate, gain_three_grad, back_local, back_prod = channel_call(
        functools.partial(gate_back_kernel, seg, width),
        [
            d_gated,
            proj_gate,
            state,
            gain_three,
            columns(inv_all),
            *[(v, width // 128) for v in d_resid_all],
            after(decay, grad_down),
        ],
        [((8 * seg, chan), LOW)] * 2 + [((8, chan), FULL)] + [channel] * 2,
        [((8 * seg, 128), FULL)],
        34,
    )
    both = [
        rows_grad(xs, [[block_pieces(v, h, seg)] for h in range(2)], 0, None, width)
        for xs, v in ((normed_in, d_proj_gate), (d_resid_all, gated))
    ]
    grad_gates = [jnp.concatenate([v[h] for v in both], axis=1) for h in range(2)]
    first_decay = by_row(decay)[:, 0]
    returned = enter(
        first_decay * by_row(back_prod)[:, 0],
        first_decay * by_row(back_local)[:, 0],
        segments,
        True,
        [],
    )

    def chip_sum(own, other):
        return (own.astype(FULL) + swap_core(other).astype(FULL)).astype(LOW)

    grad_gates = chip_sum(*grad_gates)
    mlp_places = rows_by_place(jnp.concatenate([grad_mlp, grad_down], axis=1), batch)
    returned = after(returned, grad_gates, *mlp_places, *out_sums)
    grad_gates = scatter_width(grad_gates)
    *d_scan, bound_grad = channel_call(
        functools.partial(scan_back_kernel, seg),
        [
            back_local,
            back_prod,
            returned,
            state,
            carry_in,
            proj_in,
            proj_forget,
            bound,
            keep_mask,
        ],
        [((8 * seg, chan), LOW), ((8 * seg, chan), LOW), ((8, chan), FULL)],
        (),
        0,
    )
    grad_scan = rows_grad(
        normed_in, [[block_pieces(v, h, seg) for v in d_scan] for h in range(2)], 0
    )
    grad_scan = chip_sum(*grad_scan)
    d_scan[0] = after(d_scan[0], grad_scan)
    grad_scan = scatter_width(grad_scan)
    in_parts = [(d_scan[k], (2, h), w_scan[h], k * chan) for h in range(2) for k in range(2)]
    in_parts += [(d_proj_gate, (2, h), w_gates[h], 0) for h in range(2)]
    in_sums, sent = scatter_rows(two_step(in_parts, 20, True), (grad_gates,))
    behind = settled(*sent)
    mlp = exchange(list(lax.optimization_barrier((*mlp_places, behind))[:4]))
    grad_own, gain_one_sum = token_call(
        d_in_kernel,
        [*in_sums, tok_own, inv_one, gain_one, d_resid],
        [(whole, FULL), ((1, width), FULL)],
        seg,
        width,
        0,
    )
    mixer = exchange(rows_by_place(jnp.concatenate([grad_scan, grad_gates], axis=1), batch))

    def own_rest(v):
        return (
            lax.dynamic_index_in_dim(v, core, 0, keepdims=False),
            lax.dynamic_index_in_dim(v, 1 - core, 0, keepdims=False),
        )

    (out_own,) = token_call(out_kernel, [*out_sums, after(resid, grad_own)], [(whole, LOW)], seg, width)
    out_keep, out_send = own_rest(jnp.stack([out_own[:, :half], out_own[:, half:]]))
    tokens_out = both_rows(core, out_keep, swap_core(out_send))

    gains = jnp.concatenate([gain_one_sum, gain_two_sum]).reshape(2, 2, half)
    gains_keep, gains_send = own_rest(jnp.swapaxes(gains, 0, 1))
    channels = lax.dynamic_update_slice_in_dim(
        jnp.zeros((2, 2, half), FULL),
        jnp.sum(jnp.stack([gain_three_grad, bound_grad]).reshape(2, 4, 2, chan), axis=1).swapaxes(0, 1),
        batch * chan,
        2,
    )
    small = jnp.concatenate([gains_keep, channels[0]]) + swap_core(
        jnp.concatenate([gains_send, channels[1]])
    )
    small = sum_all(after(small, *mlp, *mixer), segments)
    soft = jax.nn.softmax(bound_param, axis=0)
    grad_table = small[3] * soft * (used - jnp.sum(soft * used, axis=0))
    *grads, grad_tokens = final(
        batch, core, mlp, mixer, grad_own, swap_core(grad_own), half, 4 * unit, (behind,)
    )
    return (tokens_out, grad_tokens, *grads, small[0], small[1], small[2], grad_table)


def solution(mesh):
    return jax.shard_map(
        shards,
        mesh=mesh,
        in_specs=(
            P("batch", "seq", None),
            P("batch", "seq", None),
            P(("seq", "batch"), "mp"),
            P(("seq", "batch"), "mp"),
            P(("seq", "batch"), "mp"),
            P("mp", ("seq", "batch")),
            P(("seq", "batch"), "mp"),
            P(("seq", "batch"), "mp"),
            P("mp", ("seq", "batch")),
            P(),
            P(),
            P("mp"),
            P(None, "mp"),
            P(),
            P("batch", None),
        ),
        out_specs=(
            P("batch", "seq", "mp"),
            P("batch", "seq", None),
            P(("seq", "batch"), "mp"),
            P(("seq", "batch"), "mp"),
            P(("seq", "batch"), "mp"),
            P("mp", ("seq", "batch")),
            P(("seq", "batch"), "mp"),
            P(("seq", "batch"), "mp"),
            P("mp", ("seq", "batch")),
            P("mp"),
            P("mp"),
            P("mp"),
            P(None, "mp"),
        ),
        check_vma=False,
    )
```

```python
import functools

import jax
import jax.numpy as jnp
from jax import lax
from jax.experimental import pallas as pl
from jax.experimental.pallas import tpu as pltpu
from jax.sharding import PartitionSpec as P

EPSILON = 1e-06
LOW = jnp.bfloat16
FULL = jnp.float32
VMEM_BYTES = 56 * 1024 * 1024
ANYWHERE = pl.BlockSpec(memory_space=pl.ANY)


def swap_x(v):
    return lax.ppermute(v, "batch", [(i, i ^ 1) for i in range(4)])


def swap_y(v):
    return lax.ppermute(v, "batch", [(i, i ^ 2) for i in range(4)])


def swap_xy(v):
    return lax.ppermute(v, "batch", [(i, i ^ 3) for i in range(4)])


def swap_core(v):
    return lax.ppermute(v, "mp", [(0, 1), (1, 0)])


def after(v, *first):
    return lax.optimization_barrier((v, *first))[0]


def settled(*first):
    return swap_core(lax.optimization_barrier(first)[0][:16, :128])


def contract(left, right, left_dim, right_dim):
    return lax.dot_general(
        left, right, (((left_dim,), (right_dim,)), ((), ())), preferred_element_type=FULL
    )


def by_place(blocks, batch):
    stacked = jnp.stack(blocks)
    return [
        lax.dynamic_index_in_dim(stacked, jnp.bitwise_xor(batch, a), 0, keepdims=False)
        for a in range(4)
    ]


def exchange(blocks):
    return [blocks[0], swap_x(blocks[1]), swap_y(blocks[2]), swap_xy(blocks[3])]


def hidden_blocks(weights, batch):
    places = [
        jnp.concatenate(
            [w[:, a * (w.shape[1] // 4) : (a + 1) * (w.shape[1] // 4)] for w in weights], axis=1
        )
        for a in range(4)
    ]
    return lax.optimization_barrier(exchange(by_place(places, batch)))


def gather_width(shard):
    return lax.all_gather(shard, "seq", axis=0, tiled=True)


def shard_of(blocks, batch):
    return jnp.concatenate(by_place(blocks, batch), axis=0)


def scatter_width(grad):
    return lax.psum_scatter(grad, "seq", scatter_dimension=0, tiled=True)


def rows_by_place(part, batch):
    rows = part.shape[0] // 4
    return by_place([part[a * rows : (a + 1) * rows] for a in range(4)], batch)


def gather_rows(own, then=(), between=()):
    first, last = own
    late_first, late_last = lax.optimization_barrier((first, last, *between))[:2]
    x_first, y_last, x_last, y_first = lax.optimization_barrier(
        (swap_x(first), swap_y(last), swap_x(late_last), swap_y(late_first), *then)
    )[:4]
    d_first, d_last = lax.optimization_barrier((swap_y(x_first), swap_x(y_last)))
    return [first, last, x_first, x_last, y_first, y_last, d_first, d_last]


def scatter_rows(terms, then=()):
    mine, x_first, x_last, y_first, y_last, d_first, d_last = terms
    by_x, by_y, gx_first, gy_last = lax.optimization_barrier(
        (swap_x(d_first), swap_y(d_last), swap_x(x_first), swap_y(y_last), *then)
    )[:4]
    x_last = (x_last + by_y.astype(FULL)).astype(LOW)
    y_first = (y_first + by_x.astype(FULL)).astype(LOW)
    gx_last, gy_first = lax.optimization_barrier((swap_x(x_last), swap_y(y_first)))
    return [mine, gx_first, gx_last, gy_first, gy_last], (x_last, y_first)


def sum_tokens(v):
    got = swap_x(v)
    v = v + jnp.stack([got[1], got[0], got[3], got[2]])
    got = swap_y(v)
    return v + jnp.stack([got[2], got[3], got[0], got[1]])


def sum_all(v, count):
    v = (v + swap_x(v)) + (swap_y(v) + swap_xy(v))
    step = 1
    while step < count:
        got = [
            lax.ppermute(v, "seq", [(i, i ^ (k * step)) for i in range(count)])
            for k in (1, 2, 3)
            if k * step < count
        ]
        v = v + got[0] if len(got) < 3 else (v + got[0]) + (got[1] + got[2])
        step *= 4
    return v


def enter(product, last, count, back, hops):
    def shift(pair, k):
        hops = [(i, i + k) for i in range(count - k)]
        return lax.ppermute(pair, "seq", [(b, a) for a, b in hops] if back else hops)

    def link(earlier, later):
        return jnp.stack([earlier[0] * later[0], later[0] * earlier[1] + later[1]])

    ends = jnp.stack([product, last])
    value = shift(ends, 1)
    hops.append(value)
    step = 2
    while step < count:
        value = link(shift(link(value, ends), step), value)
        step *= 2
    return value[1]


def call(kernel, arrays, outs, scratch, cost, first=()):
    count = len(arrays)
    arrays = [*arrays, *first]

    def body(*refs):
        kernel(*refs[:count], *refs[len(arrays) :])

    return pl.pallas_call(
        body,
        in_specs=[ANYWHERE] * len(arrays),
        out_specs=[ANYWHERE] * len(outs),
        out_shape=[jax.ShapeDtypeStruct(shape, kind) for shape, kind in outs],
        scratch_shapes=[
            pltpu.SemaphoreType.DMA(v) if isinstance(v[0], int) else pltpu.VMEM(*v) for v in scratch
        ],
        compiler_params=pltpu.CompilerParams(vmem_limit_bytes=VMEM_BYTES),
        cost_estimate=pl.CostEstimate(
            flops=int(cost * 1.1e9), bytes_accessed=0, transcendentals=0
        ),
    )(*arrays)


def copy_in(source, target, sem):
    copy = pltpu.make_async_copy(source, target, sem)
    copy.start()
    return copy


def wait_all(copies):
    for copy in copies:
        copy.wait()


def dot_kernel(n, first, wide, *refs):
    xs, ws, out, (x_s, w_s, o_s, x_sem, w_sem, out_sem) = (
        refs[: 2 * n],
        refs[2 * n : 2 * n + 2],
        refs[2 * n + 2],
        refs[2 * n + 3 :],
    )
    rows = x_s.shape[1] // 2
    cols = pl.ds(first, wide)
    loads_w = [copy_in(ws[0].at[:, cols], w_s.at[0], w_sem.at[0])]
    loads = []
    for p, x in enumerate(xs):
        x = x.at[:, pl.ds(0, x_s.shape[2])]
        loads.append(copy_in(x, x_s.at[p // 2, pl.ds(p % 2 * rows, rows)], x_sem.at[p]))
        if p == 1:
            loads_w.append(copy_in(ws[1].at[:, cols], w_s.at[1], w_sem.at[1]))
    stores = []
    for r in range(n):
        wait_all(loads[2 * r : 2 * r + 2])
        for h in range(2):
            if r == 0:
                loads_w[h].wait()
            o_s[2 * r + h] = contract(x_s[r], w_s[h], 1, 0)
            at = pl.ds((2 * r + h) * 2 * rows, 2 * rows)
            stores.append(copy_in(o_s.at[2 * r + h], out.at[at], out_sem.at[2 * r + h]))
    wait_all(stores)


def rows_dot(xs, ws, first, wide, cost=0, behind=()):
    n, rows, depth = len(xs) // 2, xs[0].shape[0], ws[0].shape[0]
    return call(
        functools.partial(dot_kernel, n, first, wide),
        [*xs, *ws],
        [((4 * n * rows, wide), FULL)],
        [
            ((n, 2 * rows, depth), LOW),
            ((2, depth, wide), LOW),
            ((2 * n, 2 * rows, wide), FULL),
            (2 * n,),
            (2,),
            (2 * n,),
        ],
        cost,
        behind,
    )[0]


def acts_kernel(n, *refs):
    xs, w, outs, held, (x_s, w_s, sem, out_sem) = (
        refs[: 2 * n],
        refs[2 * n],
        refs[2 * n + 1 : 2 * n + 4],
        refs[2 * n + 4 : 2 * n + 7],
        refs[2 * n + 7 :],
    )
    rows, unit = x_s.shape[1] // 2, held[0].shape[1]
    load_w = copy_in(w, w_s, sem.at[2 * n])
    loads = [
        copy_in(x, x_s.at[p // 2, pl.ds(p % 2 * rows, rows)], sem.at[p]) for p, x in enumerate(xs)
    ]
    load_w.wait()
    stores = []
    for r in range(n):
        wait_all(loads[2 * r : 2 * r + 2])
        acts = contract(x_s[r], w_s[...], 1, 0)
        g, u = acts[:, :unit], acts[:, unit:]
        at = pl.ds(r * 2 * rows, 2 * rows)
        held[0][at, :] = g
        held[1][at, :] = u
        held[2][at, :unit] = (g * jax.nn.sigmoid(g) * u).astype(LOW)
        held[2][at, unit:] = jnp.zeros((2 * rows, held[2].shape[1] - unit), LOW)
        for k in range(3):
            stores.append(copy_in(held[k].at[at], outs[k].at[at], out_sem.at[r, k]))
    wait_all(stores)


def rows_acts(xs, w):
    n, (rows, depth), unit = len(xs) // 2, xs[0].shape, w.shape[1] // 2
    padded = pl.cdiv(unit, 128) * 128
    outs = [((2 * n * rows, v), kind) for v, kind in ((unit, FULL), (unit, FULL), (padded, LOW))]
    return call(
        functools.partial(acts_kernel, n),
        [*xs, w],
        outs,
        [*outs, ((n, 2 * rows, depth), LOW), (w.shape, LOW), (2 * n + 1,), (n, 3)],
        0,
    )


def grad_kernel(x_at, y_at, more, *refs):
    n = len(y_at)
    outs, (x_s, y_s, m_s), held = refs[-5 - 2 * n - 2 : -5 - n - 2], refs[-5 - n - 2 : -4 - n], refs[-4 - n : -4]
    x_sem, y_sem, m_sem, out_sem = refs[-4:]
    wide = held[0].shape[1]
    chunks = [chunk for group in y_at for chunk in group]
    each = y_s.shape[1] // len(chunks)
    loads = []
    for g, (target, places) in enumerate(((x_s, x_at), *[(y_s, v) for v in chunks])):
        start = 0
        for k, (i, first, rows) in enumerate(places):
            at = target.at[pl.ds(start, rows)]
            if g:
                at = target.at[pl.ds(start, rows), pl.ds((g - 1) * each, each)]
            sem = y_sem.at[g - 1, k] if g else x_sem.at[k]
            source = refs[i].at[pl.ds(first, rows), pl.ds(0, at.shape[1])]
            loads.append(copy_in(source, at, sem))
            start += rows
    if more is not None:
        load_more = copy_in(refs[more], m_s, m_sem.at[0])
    wait_all(loads)
    depth, stores = x_s.shape[1], []
    for block, first in enumerate(range(0, depth, 256)):
        cols = pl.ds(first, min(256, depth - first))
        total = contract(x_s[:, cols], y_s[...], 0, 0)
        if more is not None:
            if block == 0:
                load_more.wait()
            total = total + m_s[cols, :].astype(FULL)
        for g in range(n):
            held[g][cols, :] = total[:, g * wide : (g + 1) * wide].astype(LOW)
            stores.append(copy_in(held[g].at[cols], outs[g].at[cols], out_sem.at[g, block]))
    wait_all(stores)


def rows_grad(xs, groups, cost, more=None, depth=None):
    arrays, x_at, y_at = list(xs), [(k, 0, x.shape[0]) for k, x in enumerate(xs)], []
    for group in groups:
        y_at.append([])
        for chunk in group:
            y_at[-1].append([])
            for v, first, rows in chunk:
                found = [k for k, other in enumerate(arrays) if other is v]
                if not found:
                    found = [len(arrays)]
                    arrays.append(v)
                y_at[-1][-1].append((found[0], first, rows))
    count = sum(rows for _, _, rows in x_at)
    depth = depth or xs[0].shape[1]
    n, each = len(groups), groups[0][0][0][0].shape[1]
    wide = each * len(groups[0])
    at = None
    if more is not None:
        at = len(arrays)
        arrays.append(more)
    outs = [((depth, wide), LOW)] * n
    return call(
        functools.partial(grad_kernel, x_at, y_at, at),
        arrays,
        outs,
        [
            ((count, depth), LOW),
            ((count, n * wide), LOW),
            ((depth if more is not None else 16, wide), LOW),
            *outs,
            (len(x_at),),
            (n * len(groups[0]), len(y_at[0][0])),
            (1,),
            (n, pl.cdiv(depth, 256)),
        ],
        cost,
    )


def block_pieces(v, half, seg):
    return [(v, (2 * r + half) * seg, seg) for r in range(4)]


PIECES = (((0, 2, FULL),), ((0, 1, LOW), (1, 2, FULL)), ((0, 1, FULL), (1, 2, LOW)), ((0, 1, LOW), (1, 2, LOW)))


def term_outs(picked, seg, wide):
    return [
        (((b - a) * seg // 2, wide), kind) for r in picked for a, b, kind in PIECES[r]
    ]


def store_term(term, r, seg, held, outs, sem, start):
    stores = []
    for k, (a, b, kind) in enumerate(PIECES[r]):
        held[start + k][...] = term[a * seg // 2 : b * seg // 2].astype(kind)
        stores.append(copy_in(held[start + k], outs[start + k], sem.at[start + k]))
    return stores


def term_kernel(picked, parts, count, *refs):
    n = sum(len(PIECES[r]) for r in picked)
    arrays, outs, held = refs[:count], refs[count : count + n], refs[count + n : count + 2 * n]
    scratch = refs[count + 2 * n :]
    l_s, w_s = scratch[: len(parts)], scratch[len(parts) : 2 * len(parts)]
    l_sem, w_sem, out_sem = scratch[2 * len(parts) :]
    seg = l_s[0].shape[1]
    loads, loads_w = [], []
    for k, r in enumerate(picked):
        loads.append([])
        for p, (left, (each, half), w, first, depth) in enumerate(parts):
            if k == 0:
                source = arrays[w].at[:, pl.ds(first, depth)]
                loads_w.append(copy_in(source, w_s[p], w_sem.at[p]))
            at = pl.ds((each * r + half) * seg, seg)
            loads[k].append(copy_in(arrays[left].at[at], l_s[p].at[k], l_sem.at[k, p]))
    stores, start = [], 0
    for k, r in enumerate(picked):
        term = None
        for p in range(len(parts)):
            loads[k][p].wait()
            if k == 0:
                loads_w[p].wait()
            part = contract(l_s[p][k], w_s[p][...], 1, 1)
            term = part if term is None else term + part
        stores += store_term(term, r, seg, held, outs, out_sem, start)
        start += len(PIECES[r])
    wait_all(stores)


def rows_terms(parts, picked, seg, first=(), cost=0):
    arrays, places = [], []
    for left, block, w, column in parts:
        at = []
        for v in (left, w):
            found = [k for k, other in enumerate(arrays) if other is v]
            if not found:
                found = [len(arrays)]
                arrays.append(v)
            at.append(found[0])
        places.append((at[0], block, at[1], column, left.shape[1]))
    wide = parts[0][2].shape[0]
    outs = term_outs(picked, seg, wide)
    return call(
        functools.partial(term_kernel, picked, places, len(arrays)),
        arrays,
        outs,
        [
            *outs,
            *[((len(picked), seg, depth), LOW) for *_, depth in places],
            *[((wide, depth), LOW) for *_, depth in places],
            (len(picked), len(parts)),
            (len(parts),),
            (len(outs),),
        ],
        cost,
        first,
    )


def back_kernel(picked, *refs):
    n = len(picked)
    m = sum(len(PIECES[r]) for r in picked)
    dys, gates, ups, downs, mlps, d_acts = (
        refs[: 2 * n],
        refs[2 * n : 2 * n + 2],
        refs[2 * n + 2 : 2 * n + 4],
        refs[2 * n + 4 : 2 * n + 6],
        refs[2 * n + 6 : 2 * n + 8],
        refs[2 * n + 8],
    )
    outs, held = refs[2 * n + 9 : 2 * n + 9 + m], refs[2 * n + 9 + m : 2 * n + 9 + 2 * m]
    y_s, g_s, u_s, down_s, mlp_s, a_s, y_sem, act_sem, w_sem, a_sem, out_sem = refs[
        2 * n + 9 + 2 * m :
    ]
    seg, unit = g_s.shape[2:]
    loads_w, loads_y, loads_act = [], [], []
    for k, r in enumerate(picked):
        at = pl.ds(r * seg, seg)
        loads_y.append(
            [
                copy_in(
                    dys[2 * k + p], y_s.at[k, pl.ds(p * seg // 2, seg // 2)], y_sem.at[k, p]
                )
                for p in range(2)
            ]
        )
        loads_act.append([])
        for h in range(2):
            if k == 0:
                loads_w.append(copy_in(downs[h], down_s.at[h], w_sem.at[h, 0]))
            loads_act[k].append(
                [
                    copy_in(gates[h].at[at], g_s.at[k, h], act_sem.at[k, h, 0]),
                    copy_in(ups[h].at[at], u_s.at[k, h], act_sem.at[k, h, 1]),
                ]
            )
            if k == 0:
                loads_w.append(copy_in(mlps[h], mlp_s.at[h], w_sem.at[h, 1]))
    stores, start = [], 0
    for k, r in enumerate(picked):
        wait_all(loads_y[k])
        term = None
        for h in range(2):
            if k == 0:
                loads_w[2 * h].wait()
            d_hidden = contract(y_s[k], down_s[h], 1, 0)[:, :unit]
            wait_all(loads_act[k][h])
            g, u = g_s[k, h], u_s[k, h]
            sig = jax.nn.sigmoid(g)
            a_s[k, h, :, :unit] = (d_hidden * u * sig * (1.0 + g * (1.0 - sig))).astype(LOW)
            a_s[k, h, :, unit:] = (d_hidden * (g * sig)).astype(LOW)
            at = pl.ds((2 * k + h) * seg, seg)
            stores.append(copy_in(a_s.at[k, h], d_acts.at[at], a_sem.at[k, h]))
            if k == 0:
                loads_w[2 * h + 1].wait()
            part = contract(a_s[k, h], mlp_s[h], 1, 1)
            term = part if term is None else term + part
        stores += store_term(term, r, seg, held, outs, out_sem, start)
        start += len(PIECES[r])
    wait_all(stores)


def rows_back(dys, gates, ups, downs, mlps, picked, seg, cost):
    n, (wide, both) = len(picked), mlps[0].shape
    unit = both // 2
    outs = term_outs(picked, seg, wide)
    return call(
        functools.partial(back_kernel, picked),
        [*[dys[2 * r + p] for r in picked for p in range(2)], *gates, *ups, *downs, *mlps],
        [((2 * n * seg, both), LOW), *outs],
        [
            *outs,
            ((n, seg, wide), LOW),
            ((n, 2, seg, unit), FULL),
            ((n, 2, seg, unit), FULL),
            ((2, *downs[0].shape), LOW),
            ((2, wide, both), LOW),
            ((n, 2, seg, both), LOW),
            (n, 2),
            (n, 2, 2),
            (2, 2),
            (n, 2),
            (len(outs),),
        ],
        cost,
    )


def channel_call(kernel, arrays, outs, scratch=(), cost=0):
    def spec(shape, skip=0):
        if shape[1] == 1:
            return pl.BlockSpec(shape, lambda i: (0, 0))
        if skip == shape[1] // 128 - 1:
            return pl.BlockSpec((shape[0], 128), lambda i: (0, skip))
        return pl.BlockSpec((shape[0], 128), lambda i: (0, i + skip))

    skips = [v[1] if isinstance(v, tuple) else 0 for v in arrays]
    arrays = [v[0] if isinstance(v, tuple) else v for v in arrays]

    return pl.pallas_call(
        kernel,
        grid=(2,),
        in_specs=[spec(v.shape, skip) for v, skip in zip(arrays, skips)],
        out_specs=[spec(shape) for shape, _ in outs],
        out_shape=[jax.ShapeDtypeStruct(shape, kind) for shape, kind in outs],
        scratch_shapes=[pltpu.VMEM(*v) for v in scratch],
        compiler_params=pltpu.CompilerParams(vmem_limit_bytes=VMEM_BYTES),
        cost_estimate=pl.CostEstimate(
            flops=int(cost * 1.1e9), bytes_accessed=0, transcendentals=0
        ),
    )(*arrays)


def forward_scan(seg, rows, decay_ref, input_ref, state_ref, product_ref):
    def body(t, carry):
        h, p = carry
        at = pl.ds(t, rows, stride=seg)
        d = decay_ref[at, :]
        h = d * h + input_ref[at, :]
        p = d * p
        state_ref[at, :] = h
        product_ref[at, :] = p
        return h, p

    first = pl.ds(0, rows, stride=seg)
    h, p = input_ref[first, :], decay_ref[first, :]
    state_ref[first, :] = h
    product_ref[first, :] = p
    lax.fori_loop(1, seg, body, (h, p), unroll=5)


def backward_scan(seg, rows, decay_ref, input_ref, state_ref, product_ref):
    def body(k, carry):
        h, p, d = carry
        at = pl.ds(seg - 1 - k, rows, stride=seg)
        h = d * h + input_ref[at, :]
        p = d * p
        state_ref[at, :] = h
        product_ref[at, :] = p
        return h, p, decay_ref[at, :]

    last = pl.ds(seg - 1, rows, stride=seg)
    h, p = input_ref[last, :], decay_ref[last, :]
    state_ref[last, :] = h
    product_ref[last, :] = jnp.ones_like(p)
    at = pl.ds(seg - 2, rows, stride=seg)
    h = p * h + input_ref[at, :]
    state_ref[at, :] = h
    product_ref[at, :] = p
    lax.fori_loop(2, seg, body, (h, p, decay_ref[at, :]), unroll=2)


def scan_kernel(seg, proj_in, proj_forget, bound, keep, decay, local, product, inputs):
    rows = bound.shape[0]
    for k in range(rows):
        at = pl.ds(k * seg, seg)
        low = bound[pl.ds(k, 1), :]
        forget = low + (1.0 - low) * jax.nn.sigmoid(proj_forget[at, :])
        v = proj_in[at, :]
        decay[at, :] = forget * keep[at, :]
        inputs[at, :] = v * jax.nn.sigmoid(v) * (1.0 - forget)
    forward_scan(seg, rows, decay, inputs, local, product)


def state_kernel(seg, local, product, carry, gate, gain, state, gated, squares):
    first = pl.program_id(0) == 0
    for k in range(carry.shape[0]):
        at, one = pl.ds(k * seg, seg), pl.ds(k, 1)
        h = local[at, :] + product[at, :] * carry[one, :]
        g = gate[at, :]
        state[at, :] = h
        gated[at, :] = (h * gain[one, :] * (g * jax.nn.sigmoid(g))).astype(LOW)
        total = jnp.sum(h * h, axis=-1, keepdims=True)
        squares[at, :] = jnp.where(first, 0.0, squares[at, :]) + total


def gate_back_kernel(
    seg, wide, d_gated, gate, state, gain, inverse, *refs
):
    dots, (decay, gated, d_gate, gain_sum, local, product, held) = refs[:8], refs[8:]
    rows = gain.shape[0]
    for k in range(rows):
        at, one = pl.ds(k * seg, seg), pl.ds(k, 1)
        up, g, h, scale, inv = d_gated[at, :], gate[at, :], state[at, :], gain[one, :], inverse[at, :]
        sig = jax.nn.sigmoid(g)
        act, normed = g * sig, h * inv
        gated[at, :] = (normed * scale * act).astype(LOW)
        d_gate[at, :] = (up * normed * scale * sig * (1.0 + g * (1.0 - sig))).astype(LOW)
        gain_sum[one, :] = jnp.sum(up * normed * act, axis=0, keepdims=True)
        dot = jnp.concatenate([dots[k // 2 * 2 + p][...].astype(FULL) for p in range(2)])
        dot = jnp.sum(dot, axis=1, keepdims=True)
        shrink = inv * inv * inv * (dot * (1.0 / wide))
        held[at, :] = inv * (up * scale * act) - h * shrink
    backward_scan(seg, rows, decay, held, local, product)


def scan_back_kernel(
    seg, local, product, returned, state, carry, proj_in, proj_forget, bound, keep, d_in_ref, d_forget_ref, bound_sum
):
    for k in range(bound.shape[0]):
        at, one = pl.ds(k * seg, seg), pl.ds(k, 1)
        lam = local[at, :] + product[at, :] * returned[one, :]
        h = state[at, :]
        step = lax.broadcasted_iota(jnp.int32, h.shape, 0)
        previous = jnp.where(step == 0, carry[one, :], pltpu.roll(h, 1, 0))
        low, v = bound[one, :], proj_in[at, :]
        sig_forget, sig_in = jax.nn.sigmoid(proj_forget[at, :]), jax.nn.sigmoid(v)
        forget = low + (1.0 - low) * sig_forget
        d_forget = lam * (previous * keep[at, :] - v * sig_in)
        d_in = lam * (1.0 - forget) * sig_in * (1.0 + v * (1.0 - sig_in))
        d_in_ref[at, :] = d_in.astype(LOW)
        d_forget_ref[at, :] = (d_forget * (1.0 - low) * sig_forget * (1.0 - sig_forget)).astype(LOW)
        bound_sum[one, :] = jnp.sum(d_forget * (1.0 - sig_forget), axis=0, keepdims=True)


STEP = 32


def token_call(kernel, arrays, outs, seg, wide, cost=0):
    half = seg // 2

    def spec(shape):
        if shape[0] == 1:
            return pl.BlockSpec(shape, lambda i: (0, 0))
        if shape[0] == 2:
            return pl.BlockSpec((2, STEP, shape[2]), lambda i: (0, i, 0))
        return pl.BlockSpec((STEP, shape[1]), lambda i: (i, 0))

    def folded(shape):
        return (2, half, shape[1]) if shape[0] == seg else shape

    arrays = [v.reshape(folded(v.shape)) for v in arrays]
    got = pl.pallas_call(
        kernel,
        grid=(half // STEP,),
        in_specs=[spec(v.shape) for v in arrays],
        out_specs=[spec(folded(shape)) for shape, _ in outs],
        out_shape=[jax.ShapeDtypeStruct(folded(shape), kind) for shape, kind in outs],
        compiler_params=pltpu.CompilerParams(vmem_limit_bytes=VMEM_BYTES),
        cost_estimate=pl.CostEstimate(
            flops=int(cost * 1.1e9), bytes_accessed=0, transcendentals=0
        ),
    )(*arrays)
    return [v.reshape(shape) for v, (shape, _) in zip(got, outs)]


def both_rows(core, mine, got):
    return jnp.where(core == 0, jnp.stack([mine, got]), jnp.stack([got, mine]))


def final_kernel(place, core, *refs):
    mlp, mixer, (mine, got), refs = refs[:4], refs[4:8], refs[8:10], refs[10:]
    outs, (m_s, x_s, t_s), refs = refs[:8], refs[8:11], refs[11:]
    held, (sem, out_sem) = refs[:7], refs[7:]
    rows = [copy_in(v, t_s.at[k], sem.at[8 + k]) for k, v in enumerate((mine, got))]
    loads = [copy_in(v, m_s.at[k], sem.at[k]) for k, v in enumerate(mlp)]
    loads += [copy_in(v, x_s.at[k], sem.at[4 + k]) for k, v in enumerate(mixer)]
    wait_all(rows)
    stores = [
        copy_in(t_s.at[0], outs[7].at[core[0]], out_sem.at[7]),
        copy_in(t_s.at[1], outs[7].at[1 - core[0]], out_sem.at[8]),
    ]
    wait_all(loads)
    chan, unit = held[0].shape[1] // 4, held[4].shape[1] // 4
    for a in range(4):
        block = jnp.bitwise_xor(place[0], a)
        m, x = m_s[block].astype(FULL), x_s[block].astype(FULL)
        for k in range(3):
            held[k][:, a * chan : (a + 1) * chan] = x[:, k * chan : (k + 1) * chan]
        held[3][a * chan : (a + 1) * chan, :] = x[:, 3 * chan : 4 * chan].T
        for k in range(2):
            held[4 + k][:, a * unit : (a + 1) * unit] = m[:, k * unit : (k + 1) * unit]
        held[6][a * unit : (a + 1) * unit, :] = m[:, 2 * unit : 3 * unit].T
    stores += [copy_in(held[k], outs[k], out_sem.at[k]) for k in range(7)]
    wait_all(stores)


def final(place, core, mlp, mixer, mine, got, half, hidden, first):
    rows = mixer[0].shape[0]
    outs = [((rows, half), FULL)] * 3 + [((half, rows), FULL)]
    outs += [((rows, hidden), FULL)] * 2 + [((hidden, rows), FULL)]
    arrays = [*mlp, *mixer, mine, got, *first]
    more = [((2, *mine.shape), FULL)]

    def body(place_ref, core_ref, *refs):
        final_kernel(place_ref, core_ref, *refs[:10], *refs[len(arrays) :])

    return pl.pallas_call(
        body,
        in_specs=[pl.BlockSpec(memory_space=pltpu.SMEM)] * 2 + [ANYWHERE] * len(arrays),
        out_specs=[ANYWHERE] * 8,
        out_shape=[jax.ShapeDtypeStruct(shape, kind) for shape, kind in outs + more],
        scratch_shapes=[
            pltpu.VMEM((4, *mlp[0].shape), LOW),
            pltpu.VMEM((4, *mixer[0].shape), LOW),
            pltpu.VMEM((2, *mine.shape), FULL),
            *[pltpu.VMEM(*v) for v in outs],
            pltpu.SemaphoreType.DMA((10,)),
            pltpu.SemaphoreType.DMA((9,)),
        ],
        compiler_params=pltpu.CompilerParams(vmem_limit_bytes=VMEM_BYTES),
    )(place.reshape(1), core.reshape(1), *arrays)


def total_of(refs, h):
    mine, gx_first, gx_last, gy_first, gy_last = refs
    got_x, got_y = ((gx_first, gy_first), (gx_last, gy_last))[h]
    return mine[h] + got_x[...].astype(FULL) + got_y[...].astype(FULL)


def inverse_of(v):
    return lax.rsqrt(jnp.mean(v * v, axis=-1, keepdims=True) + EPSILON)


def enter_kernel(tok, gain, first, last, inverse):
    for h, out in enumerate((first, last)):
        v = tok[h].astype(FULL)
        inv = inverse_of(v)
        out[...] = (v * inv * gain[...]).astype(LOW)
        inverse[h] = inv


def mixed_kernel(*refs):
    *sums, tok, inv_state, gain, mix, resid, first, last, inverse = refs
    for h, out in enumerate((first, last)):
        raw = total_of(sums, h)
        v = tok[h].astype(FULL) + inv_state[h] * raw
        inv = inverse_of(v)
        mix[h] = raw
        resid[h] = v
        out[...] = (v * inv * gain[...]).astype(LOW)
        inverse[h] = inv


def norm_back(upstream, v, scale, inv):
    weighted = upstream * scale
    mean = jnp.mean(weighted * v, axis=-1, keepdims=True)
    return inv * weighted - v * (inv * inv * inv * mean)


def add_rows(ref, v):
    total = jnp.sum(v, axis=0, keepdims=True)

    @pl.when(pl.program_id(0) == 0)
    def _():
        ref[...] = jnp.zeros_like(ref)

    ref[...] += total


def d_mlp_kernel(*refs):
    *sums, resid, inverse, cot_first, cot_last, gain, mix, d_resid, first, last, gain_sum = refs
    terms = 0.0
    for h, (cot, out) in enumerate(((cot_first, first), (cot_last, last))):
        up, v, inv = total_of(sums, h), resid[h], inverse[h]
        terms = terms + up * v * inv
        grad = cot[...].astype(FULL) + norm_back(up, v, gain[...], inv)
        low = grad.astype(LOW)
        d_resid[h] = grad
        wide = low.shape[1]
        out[:, :wide] = low
        dot = jnp.sum(low.astype(FULL) * mix[h], axis=-1, keepdims=True)
        high = dot.astype(LOW)
        dot = dot - high.astype(FULL)
        middle = dot.astype(LOW)
        rest = (dot - middle.astype(FULL)).astype(LOW)
        lane = lax.broadcasted_iota(jnp.int32, (low.shape[0], 128), 1)
        parts = jnp.where(lane == 1, middle.astype(FULL), jnp.where(lane == 2, rest.astype(FULL), 0.0))
        out[:, wide:] = jnp.where(lane == 0, high.astype(FULL), parts).astype(LOW)
    add_rows(gain_sum, terms)


def d_in_kernel(*refs):
    *sums, tok, inverse, gain, d_resid, grad, gain_sum = refs
    terms = 0.0
    for h in range(2):
        up, v, inv = total_of(sums, h), tok[h].astype(FULL), inverse[h]
        terms = terms + up * v * inv
        grad[h] = d_resid[h] + norm_back(up, v, gain[...], inv)
    add_rows(gain_sum, terms)


def out_kernel(*refs):
    *sums, resid, out = refs
    for h in range(2):
        out[h] = (resid[h] + total_of(sums, h)).astype(LOW)


def shards(
    tokens_in,
    grad_out,
    w_input,
    w_forget,
    w_outgate,
    w_out,
    mlp_gate,
    mlp_up,
    mlp_down,
    gain_mixer,
    gain_mlp,
    gain_state,
    bound_param,
    layer_index,
    doc_lengths,
):
    rows, seg, width = tokens_in.shape
    half = gain_state.shape[0]
    chan = half // 4
    unit = mlp_gate.shape[1] // 4
    segments = lax.axis_size("seq")
    core = lax.axis_index("mp")
    batch = lax.axis_index("batch")
    place = lax.axis_index("seq")
    piece = (seg // 2, width)
    wider = (seg // 2, width + 128)
    whole = (seg, width)
    column = (seg, 1)

    def own_other(v):
        return [v, swap_core(v)]

    mixer = hidden_blocks((w_input, w_forget, w_outgate, w_out.T), batch)
    shard = shard_of(mixer, batch)
    w_scan, w_gates = gather_width(shard[:, : 2 * chan]), gather_width(shard[:, 2 * chan :])
    layers = bound_param.shape[0]
    layer = jnp.arange(layers, dtype=jnp.int32)[:, None]
    used = jnp.logical_and(layer >= 1, layer <= layer_index[0]).astype(FULL)
    table = jnp.concatenate([bound_param, gain_state.astype(FULL)[None]])
    table = jnp.stack(own_other(lax.dynamic_slice_in_dim(table, batch * chan, chan, 1)))
    bound = jnp.tile(jnp.sum(jax.nn.softmax(table[:, :layers], axis=1) * used, axis=1), (4, 1))
    gain_three = jnp.tile(table[:, layers], (4, 1))
    lengths = lax.dynamic_slice_in_dim(doc_lengths, core, 1, 0)
    lengths = jnp.concatenate([lengths, swap_x(lengths)])
    lengths = jnp.concatenate([lengths, swap_y(lengths)])
    starts = jnp.cumsum(lengths, axis=1) - lengths
    places = place * seg + jnp.arange(seg, dtype=jnp.int32)
    resets = jnp.any(places[None, :, None] == starts[:, None, :], axis=2).astype(FULL)
    keep_mask = jnp.repeat(1.0 - resets, 2, axis=0).reshape(8 * seg, 1)
    mlp_blocks = hidden_blocks((after(mlp_gate, lengths, table, *mixer), mlp_up, mlp_down.T), batch)
    shard = shard_of(mlp_blocks, batch)
    w_mlp, down = gather_width(shard[:, : 2 * unit]), shard[:, 2 * unit :]
    down = jnp.pad(down, ((0, 0), (0, -unit % 128)))

    gain_one = gain_mixer.astype(FULL)[None]
    gain_two = gain_mlp.astype(FULL)[None]
    tok_own, cot_own = lax.optimization_barrier(
        [lax.dynamic_index_in_dim(v, core, 0, keepdims=False) for v in (tokens_in, grad_out)]
    )

    def by_row(v):
        return v.reshape(8, seg, chan)

    def columns(v):
        return jnp.repeat(v, 2, axis=0).reshape(8 * seg, 1)

    channel = ((8 * seg, chan), FULL)

    *normed, inv_one = token_call(
        enter_kernel,
        [tok_own, gain_one],
        [(piece, LOW), (piece, LOW), (column, FULL)],
        seg,
        width,
    )
    normed = lax.optimization_barrier((*normed, *mixer))[:2]
    normed_in = gather_rows(normed, (), mlp_blocks)
    w_scan = own_other(after(w_scan, normed_in[6]))
    proj_scan = rows_dot(normed_in, w_scan, 0, 2 * chan, 0)
    proj_in, proj_forget = (proj_scan, 0), (proj_scan, chan // 128)
    decay, local_state, cum_decay = channel_call(
        functools.partial(scan_kernel, seg),
        [proj_in, proj_forget, bound, keep_mask],
        [channel] * 3,
        [((8 * seg, 128), FULL)],
    )
    w_gates = own_other(after(w_gates, local_state))
    hops = []
    carry_in = enter(by_row(cum_decay)[:, -1], by_row(local_state)[:, -1], segments, False, hops)
    cot_pieces = [cot_own[: seg // 2], cot_own[seg // 2 :]]
    proj_gate = rows_dot(normed_in, w_gates, 0, chan, 0, (hops[0].reshape(-1, chan),))
    carry_in = after(carry_in, proj_gate)
    state, gated_raw, squares = channel_call(
        functools.partial(state_kernel, seg),
        [local_state, cum_decay, carry_in, proj_gate, gain_three],
        [channel, ((8 * seg, chan), LOW), ((8 * seg, 1), FULL)],
    )
    square_total = sum_tokens(jnp.sum(squares.reshape(4, 2, seg), axis=1))
    inv_all = lax.rsqrt(square_total / width + EPSILON)
    inv_own = inv_all[0][:, None]
    gated_raw = after(gated_raw, square_total)

    def two_step(parts, cost=0, behind=False):
        diag = rows_terms(parts, (3,), seg, cost=cost)
        first = settled(*diag) if behind else diag[0]
        rest = rows_terms(parts, (1, 2, 0), seg, (first,))
        return [rest[4], *rest[:4], *diag]

    mix_parts = [(gated_raw, (2, h), w_gates[h], chan) for h in range(2)]
    mix_sums, _ = scatter_rows(two_step(mix_parts))
    mix_raw, resid, *normed, inv_two = token_call(
        mixed_kernel,
        [*mix_sums, tok_own, inv_own, gain_two],
        [(whole, FULL), (whole, FULL), (piece, LOW), (piece, LOW), (column, FULL)],
        seg,
        width,
    )

    normed_mlp = gather_rows(normed)
    cot_pieces = lax.optimization_barrier((*cot_pieces, normed_mlp[6]))[:2]
    w_mlp = own_other(after(w_mlp, normed_mlp[2]))
    acts = [rows_acts(normed_mlp, w) for w in w_mlp]
    gate_act, up_act, hidden = zip(*acts)
    cot_all = gather_rows(cot_pieces, (hidden[1],))

    def hidden_pieces(h):
        return [(hidden[h], r * seg, seg) for r in range(4)]

    (grad_other,) = rows_grad(cot_all, [[hidden_pieces(1)]], 0)
    (grad_down,) = rows_grad(cot_all, [[hidden_pieces(0)]], 0, swap_core(grad_other))
    w_down = gather_width(after(down, normed_mlp[2]))
    w_down = own_other(after(w_down, *hidden))
    w_down[0] = after(w_down[0], grad_other)
    grad_down = scatter_width(grad_down)
    d_acts = {}

    def back_terms(picked, cost, *first):
        downs = [after(w_down[0], *first), w_down[1]] if first else w_down
        d_acts[picked], *terms = rows_back(cot_all, gate_act, up_act, downs, w_mlp, picked, seg, cost)
        return terms

    diag = back_terms((3,), 0)
    sides = back_terms((1, 2), 0, diag[0])
    mine = back_terms((0,), 0, sides[0])
    mlp_sums, sent = scatter_rows([*mine, *sides, *diag], tuple(mine))
    def d_act_pieces(h):
        return [
            (d_acts[picked], (2 * k + h) * seg, seg)
            for picked, k in (((0,), 0), ((1, 2), 0), ((1, 2), 1), ((3,), 0))
        ]

    normed_mlp[0] = after(normed_mlp[0], *sent)
    (grad_other,) = rows_grad(normed_mlp, [[d_act_pieces(1)]], 0)
    (grad_mlp,) = rows_grad(normed_mlp, [[d_act_pieces(0)]], 0, swap_core(grad_other))
    mlp_sums[0] = after(mlp_sums[0], grad_mlp)

    d_resid, *d_low, gain_two_sum = token_call(
        d_mlp_kernel,
        [*mlp_sums, resid, inv_two, *cot_all[:2], gain_two, mix_raw],
        [(whole, FULL), (wider, LOW), (wider, LOW), ((1, width), FULL)],
        seg,
        width,
        14,
    )
    hidden = [after(hidden[0], *d_low), hidden[1]]
    out_terms = two_step([(hidden[h], (1, 0), w_down[h], 0) for h in range(2)], 0)
    d_resid_all = gather_rows(d_low)
    d_resid_all[6] = after(d_resid_all[6], grad_mlp, *out_terms)
    grad_mlp = scatter_width(grad_mlp)
    out_terms = list(lax.optimization_barrier((*out_terms, d_resid_all[6]))[:-1])
    out_sums, sent = scatter_rows(out_terms)
    d_gated = rows_dot(d_resid_all, w_gates, chan, chan, 21)
    gated, d_proj_gate, gain_three_grad, back_local, back_prod = channel_call(
        functools.partial(gate_back_kernel, seg, width),
        [
            d_gated,
            proj_gate,
            state,
            gain_three,
            columns(inv_all),
            *[(v, width // 128) for v in d_resid_all],
            after(decay, grad_down),
        ],
        [((8 * seg, chan), LOW)] * 2 + [((8, chan), FULL)] + [channel] * 2,
        [((8 * seg, 128), FULL)],
        34,
    )
    both = [
        rows_grad(xs, [[block_pieces(v, h, seg)] for h in range(2)], 0, None, width)
        for xs, v in ((normed_in, d_proj_gate), (d_resid_all, gated))
    ]
    grad_gates = [jnp.concatenate([v[h] for v in both], axis=1) for h in range(2)]
    first_decay = by_row(decay)[:, 0]
    returned = enter(
        first_decay * by_row(back_prod)[:, 0],
        first_decay * by_row(back_local)[:, 0],
        segments,
        True,
        [],
    )

    def chip_sum(own, other):
        return (own.astype(FULL) + swap_core(other).astype(FULL)).astype(LOW)

    grad_gates = chip_sum(*grad_gates)
    mlp_places = rows_by_place(jnp.concatenate([grad_mlp, grad_down], axis=1), batch)
    returned = after(returned, grad_gates, *mlp_places, *out_sums)
    grad_gates = scatter_width(grad_gates)
    *d_scan, bound_grad = channel_call(
        functools.partial(scan_back_kernel, seg),
        [
            back_local,
            back_prod,
            returned,
            state,
            carry_in,
            proj_in,
            proj_forget,
            bound,
            keep_mask,
        ],
        [((8 * seg, chan), LOW), ((8 * seg, chan), LOW), ((8, chan), FULL)],
        (),
        0,
    )
    grad_scan = rows_grad(
        normed_in, [[block_pieces(v, h, seg) for v in d_scan] for h in range(2)], 0
    )
    grad_scan = chip_sum(*grad_scan)
    d_scan[0] = after(d_scan[0], grad_scan)
    grad_scan = scatter_width(grad_scan)
    in_parts = [(d_scan[k], (2, h), w_scan[h], k * chan) for h in range(2) for k in range(2)]
    in_parts += [(d_proj_gate, (2, h), w_gates[h], 0) for h in range(2)]
    in_sums, sent = scatter_rows(two_step(in_parts, 20, True), (grad_gates,))
    behind = settled(*sent)
    mlp = exchange(list(lax.optimization_barrier((*mlp_places, behind))[:4]))
    grad_own, gain_one_sum = token_call(
        d_in_kernel,
        [*in_sums, tok_own, inv_one, gain_one, d_resid],
        [(whole, FULL), ((1, width), FULL)],
        seg,
        width,
        0,
    )
    mixer = exchange(rows_by_place(jnp.concatenate([grad_scan, grad_gates], axis=1), batch))

    def own_rest(v):
        return (
            lax.dynamic_index_in_dim(v, core, 0, keepdims=False),
            lax.dynamic_index_in_dim(v, 1 - core, 0, keepdims=False),
        )

    (out_own,) = token_call(out_kernel, [*out_sums, after(resid, grad_own)], [(whole, LOW)], seg, width)
    out_keep, out_send = own_rest(jnp.stack([out_own[:, :half], out_own[:, half:]]))
    tokens_out = both_rows(core, out_keep, swap_core(out_send))

    gains = jnp.concatenate([gain_one_sum, gain_two_sum]).reshape(2, 2, half)
    gains_keep, gains_send = own_rest(jnp.swapaxes(gains, 0, 1))
    channels = lax.dynamic_update_slice_in_dim(
        jnp.zeros((2, 2, half), FULL),
        jnp.sum(jnp.stack([gain_three_grad, bound_grad]).reshape(2, 4, 2, chan), axis=1).swapaxes(0, 1),
        batch * chan,
        2,
    )
    small = jnp.concatenate([gains_keep, channels[0]]) + swap_core(
        jnp.concatenate([gains_send, channels[1]])
    )
    small = sum_all(after(small, *mlp, *mixer), segments)
    soft = jax.nn.softmax(bound_param, axis=0)
    grad_table = small[3] * soft * (used - jnp.sum(soft * used, axis=0))
    *grads, grad_tokens = final(
        batch, core, mlp, mixer, grad_own, swap_core(grad_own), half, 4 * unit, (behind,)
    )
    return (tokens_out, grad_tokens, *grads, small[0], small[1], small[2], grad_table)


def solution(mesh):
    return jax.shard_map(
        shards,
        mesh=mesh,
        in_specs=(
            P("batch", "seq", None),
            P("batch", "seq", None),
            P(("seq", "batch"), "mp"),
            P(("seq", "batch"), "mp"),
            P(("seq", "batch"), "mp"),
            P("mp", ("seq", "batch")),
            P(("seq", "batch"), "mp"),
            P(("seq", "batch"), "mp"),
            P("mp", ("seq", "batch")),
            P(),
            P(),
            P("mp"),
            P(None, "mp"),
            P(),
            P("batch", None),
        ),
        out_specs=(
            P("batch", "seq", "mp"),
            P("batch", "seq", None),
            P(("seq", "batch"), "mp"),
            P(("seq", "batch"), "mp"),
            P(("seq", "batch"), "mp"),
            P("mp", ("seq", "batch")),
            P(("seq", "batch"), "mp"),
            P(("seq", "batch"), "mp"),
            P("mp", ("seq", "batch")),
            P("mp"),
            P("mp"),
            P("mp"),
            P(None, "mp"),
        ),
        check_vma=False,
    )
```
